128 devices in a mesh: plane: 8 (over x, core), band: 16 (over y, z).
Axes of the slice: x: 4, y: 4, z: 4, core: 2. Of those that a mesh axis runs over, the one named last changes fastest.
Arguments:
- slabs: bfloat16 [8, 1024, 4, 8192], P('plane', 'band'), may hold values from -1 to 1
- slot_block: int32 [8, 1024], P('plane', 'band'), may hold values from 0 to 31, as said below
- lens_weight: float32 [8], P('plane'), may hold values from 0.1 to 0.4
Outputs:
- ray_state: float32 [8, 6, 128, 8192], P('plane', None, 'band')
The draws below stay inside these ranges and needn't reach their ends.
Inputs may be any that keep to these rules, and one draw needn't show every extreme that they name: `slot_block`: entry j of a device's list names the row-block that slot j adds to; the blocks of band b are b * 2 to b * 2 + 1. No device names blocks of one band in more than 8 slots, and in every plane some bands are named 8 times by every device of that plane.
All inputs are finite; a program needn't handle non-finite values.
Results may differ from the reference program's by a relative error of at most 0.006.
Values may be sent and summed in bfloat16 or wider, within the bound.
No kernel may reach another device: no remote copies, remote signals or barrier semaphores. Data moves between devices by JAX's collectives and lax.ppermute only.
A program may use at most 64 MiB of HBM per device.

```python
import math
import jax
import jax.numpy as jnp
from jax import lax

NCOL = 8192
BLK = 4
CAP = 8
SWEEPS = 20
PLANES = 8
SLOTS = 64
BPB = 2
NBLK = 32
NROW = 128
N_BAND = 16


def plan_blocks(key):
    key = jax.random.fold_in(key, 11)
    key_hot, key_noise, key_order, key_offset = jax.random.split(key, 4)
    band_ids = jnp.arange(N_BAND, dtype=jnp.int32)
    hot_score = jax.random.randint(key_hot, (PLANES, N_BAND), 0, 4096) * N_BAND + band_ids[None, :]
    hot_rank = jnp.argsort(jnp.argsort(hot_score, axis=1), axis=1)
    hot = hot_rank < N_BAND // 4
    candidate = jnp.arange(N_BAND * CAP, dtype=jnp.int32)
    cand_band = candidate // CAP
    bias = jnp.where(hot[:, cand_band], 0, 1 << 20)
    noise = jax.random.randint(key_noise, (PLANES, N_BAND, N_BAND * CAP), 0, 1024)
    score = bias[:, None, :] + noise * (N_BAND * CAP) + candidate[None, None, :]
    chosen = jnp.argsort(score, axis=-1)[:, :, :SLOTS]
    mixing = jax.random.randint(key_order, (PLANES, N_BAND, SLOTS), 0, 1024) * SLOTS + jnp.arange(SLOTS, dtype=jnp.int32)
    order = jnp.argsort(mixing, axis=-1)
    chosen = jnp.take_along_axis(chosen, order, axis=-1)
    band_sel = (chosen // CAP).astype(jnp.int32)
    offset = jax.random.randint(key_offset, (PLANES, N_BAND, SLOTS), 0, BPB)
    return (band_sel * BPB + offset).reshape(PLANES, N_BAND * SLOTS).astype(jnp.int32)


def draw_slot_block(key, part):
    return plan_blocks(key)


def draw_slabs(key, part):
    blocks = plan_blocks(key)
    key = jax.random.fold_in(key, 29)
    key_phase, key_level, key_share, key_column, key_rough = jax.random.split(key, 5)
    block_ids = jnp.arange(NBLK, dtype=jnp.int32)
    members = (blocks[:, :, None] == block_ids[None, None, :]).astype(jnp.float32)
    counts = jnp.sum(members, axis=1)
    stripe_phase = jax.random.randint(key_phase, (), 0, 4)
    stripe = block_ids * BLK // 8
    loud_block = (stripe + stripe_phase) % 4 == 0
    spread = jnp.exp(jax.random.uniform(key_level, (PLANES, NBLK), jnp.float32, jnp.log(0.7), jnp.log(1.4)))
    strength = jnp.where(loud_block[None, :], 0.8, 0.05) * spread
    rough_level = jnp.where(loud_block, 0.1, 0.01)
    slot_level = jnp.take_along_axis(strength / jnp.maximum(counts, 6.0), blocks, axis=1)
    slot_rough = rough_level[blocks]
    slot_share = jax.random.uniform(key_share, (PLANES, N_BAND * SLOTS), jnp.float32, 0.5, 1.5)
    column_phase = jax.random.uniform(key_column, (PLANES, 1), jnp.float32, 0.0, 2.0 * jnp.pi)
    columns = jnp.arange(NCOL, dtype=jnp.float32)[None, :]
    full_shape = (PLANES, N_BAND * SLOTS, BLK, NCOL)
    profile = 1.0 + 0.6 * jnp.cos(columns * (2.0 * jnp.pi / 8.0) + column_phase)
    rough_part = jax.random.truncated_normal(key_rough, -3.0, 3.0, full_shape, jnp.float32)
    coherent = (slot_level * slot_share)[:, :, None, None] * profile[:, None, None, :]
    slab_values = coherent + slot_rough[:, :, None, None] * rough_part
    return slab_values.astype(jnp.bfloat16)


def steps_of(stream_key, dims, cuts, smallest, high):
    loudness, own = 1.0, jax.random.fold_in(stream_key, 6)
    for dim, blocks in cuts:
        steps = jnp.exp(jax.random.uniform(jax.random.fold_in(own, dim), (blocks,), jnp.float32, smallest / len(cuts), high / len(cuts)))
        loudness = loudness * jnp.repeat(steps, dims[dim] // blocks).reshape([-1 if axis == dim else 1 for axis in range(len(dims))])
    return loudness


def setup_inputs(seed: int = 0) -> dict:
    key_list = jax.random.split(jax.random.key(seed), 4)
    slabs = draw_slabs(jax.random.fold_in(key_list[3], 71), 0)
    slot_block = draw_slot_block(jax.random.fold_in(key_list[3], 71), 0)
    lens_weight = jnp.clip(jnp.exp(math.log(0.4) - 1.3862944 * jax.random.uniform(key_list[2], (PLANES,), jnp.float32) ** steps_of(key_list[2], (PLANES,), ((0, 8),), -0.2, 0.2)), 0.1, 0.4)
    return dict(slabs=slabs, slot_block=slot_block, lens_weight=lens_weight)


MASS = 0.05


def sweep_once(potential, density):
    padded = jnp.pad(potential, ((1, 1), (0, 0)))
    neighbours = padded[:-2] + padded[2:] + jnp.roll(potential, 1, 1) + jnp.roll(potential, -1, 1)
    return (density + neighbours) / (4.0 + MASS)


def plane_maps(slab_plane, block_plane, weight):
    pieces = slab_plane.astype(jnp.float32)
    summed = jax.ops.segment_sum(pieces, block_plane, num_segments=NBLK)
    density = summed.reshape(NROW, NCOL)

    def body_sweep(index, potential):
        return sweep_once(potential, density)

    potential = lax.fori_loop(0, SWEEPS, body_sweep, jnp.zeros((NROW, NCOL), jnp.float32))
    padded = jnp.pad(potential, ((1, 1), (0, 0)))
    center = potential
    north = padded[2:]
    south = padded[:-2]
    east = jnp.roll(center, -1, 1)
    west = jnp.roll(center, 1, 1)
    grad_one = 0.5 * (east - west)
    grad_two = 0.5 * (north - south)
    second_one = east - 2.0 * center + west
    second_two = north - 2.0 * center + south
    mixed = 0.25 * (jnp.roll(north, -1, 1) - jnp.roll(north, 1, 1) - jnp.roll(south, -1, 1) + jnp.roll(south, 1, 1))
    return jnp.stack([1.0 - weight * second_one, -weight * mixed, 1.0 - weight * second_two,
                      weight * grad_one, weight * grad_two])


def apply_map(maps, state):
    p11, p12, p22, c1, c2 = maps[0], maps[1], maps[2], maps[3], maps[4]
    a11, a12, a21, a22, s1, s2 = state[0], state[1], state[2], state[3], state[4], state[5]
    return jnp.stack([p11 * a11 + p12 * a21, p11 * a12 + p12 * a22,
                      p12 * a11 + p22 * a21, p12 * a12 + p22 * a22,
                      p11 * s1 + p12 * s2 + c1, p12 * s1 + p22 * s2 + c2])


def reference(slabs, slot_block, lens_weight):
    ones = jnp.ones((NROW, NCOL), jnp.float32)
    zeros = jnp.zeros((NROW, NCOL), jnp.float32)
    identity_state = jnp.stack([ones, zeros, zeros, ones, zeros, zeros])
    state = identity_state
    results = []
    for plane_index in range(PLANES):
        maps = plane_maps(slabs[plane_index], slot_block[plane_index], lens_weight[plane_index])
        state = apply_map(maps, state)
        results.append(state - identity_state)
    return jnp.stack(results)
```

```python
import jax
import jax.numpy as jnp
from jax import lax
from jax.experimental import pallas as pl
from jax.experimental.pallas import tpu as pltpu
from jax.sharding import PartitionSpec as P

NCOL = 8192
NROW = 128
R = 8
BLK = 4
SLOTS = 64
SWEEPS = 20
PLANES = 8
BANDS = 16
MASS = 0.05

OWN = NCOL // BANDS
HALO = 24
SPAN = OWN + 2 * HALO
TILE = 128
ROWS = R + 2
MSG = ROWS * OWN // TILE
TOP = 14.0


def partial_kernel(slot_ref, slab_ref, out_ref, scale_ref, select_ref, most_ref):
    step = pl.program_id(0)

    @pl.when(step == 0)
    def _():
        lane = lax.broadcasted_iota(jnp.int32, (8, NROW), 1)
        sub = lax.broadcasted_iota(jnp.int32, (8, NROW), 0)
        for pair in range(SLOTS // 4):
            halves = []
            for half in range(2):
                first = 4 * pair + 2 * half
                block = jnp.where(sub < BLK, slot_ref[0, first], slot_ref[0, first + 1])
                row = block * BLK + (sub & (BLK - 1))
                halves.append(jnp.where(lane == row, 1.0, 0.0))
            select_ref[16 * pair : 16 * pair + 16] = jnp.concatenate(halves, 0).astype(jnp.bfloat16)
        most_ref[...] = jnp.zeros_like(most_ref)

    slabs = slab_ref[...].reshape(SLOTS * BLK, OWN)
    part = lax.dot_general(
        slabs, select_ref[...], (((0,), (0,)), ((), ())), preferred_element_type=jnp.float32
    )
    after = lax.rem(step + 1, BANDS)
    before = lax.rem(step + BANDS - 1, BANDS)
    out_ref[step, HALO : HALO + OWN] = part
    out_ref[after, 0:HALO] = part[OWN - HALO :]
    out_ref[before, HALO + OWN :] = part[:HALO]
    most_ref[...] = jnp.maximum(
        most_ref[...], jnp.max(jnp.abs(part).reshape(OWN // 8, 8, NROW), axis=0)
    )

    @pl.when(step == BANDS - 1)
    def _():
        most = jnp.max(most_ref[...])
        most = jnp.full((8, NROW), most, jnp.float32)
        power = jnp.ceil(jnp.log2(jnp.maximum(most, 2.0**-100)))
        scale_ref[...] = jnp.exp2(TOP - power)
        mark = power * jnp.exp2(power - TOP)
        for band in range(BANDS):
            out_ref[band, 0:1] = mark[0:1]


def partial_densities(slabs, slot_block):
    return pl.pallas_call(
        partial_kernel,
        grid=(BANDS,),
        in_specs=[
            pl.BlockSpec(memory_space=pltpu.SMEM),
            pl.BlockSpec((SLOTS, BLK, OWN), lambda step: (0, 0, step)),
        ],
        out_specs=[
            pl.BlockSpec((BANDS, SPAN, NROW), lambda step: (0, 0, 0)),
            pl.BlockSpec((8, NROW), lambda step: (0, 0)),
        ],
        out_shape=[
            jax.ShapeDtypeStruct((BANDS, SPAN, NROW), jnp.float32),
            jax.ShapeDtypeStruct((8, NROW), jnp.float32),
        ],
        scratch_shapes=[
            pltpu.VMEM((SLOTS * BLK, NROW), jnp.bfloat16),
            pltpu.VMEM((8, NROW), jnp.float32),
        ],
        compiler_params=pltpu.CompilerParams(vmem_limit_bytes=24 * 2**20),
        name="partial_densities",
    )(slot_block, slabs)


STRIP = 80


def relax_kernel(weight_ref, density_ref, out_ref, even_ref, odd_ref, turned_ref):
    zero = jnp.zeros((8, NROW), jnp.float32)
    for ref in (even_ref, odd_ref):
        ref[0:8] = zero
        ref[8 + SPAN :] = zero
    turned_ref[0:8] = zero
    turned_ref[8 + NROW :] = zero
    lane = lax.broadcasted_iota(jnp.int32, (STRIP, NROW), 1)
    not_first = lane > 0
    not_last = lane < NROW - 1
    share = 1.0 / (4.0 + MASS)
    even_ref[8 : 8 + SPAN] = density_ref[...] * share

    def sweep(src, dst):
        for start in range(8, 8 + SPAN, STRIP):
            here = src[start : start + STRIP]
            total = src[start - 1 : start - 1 + STRIP] + src[start + 1 : start + 1 + STRIP]
            total += jnp.where(not_first, pltpu.roll(here, 1, 1), 0.0)
            total += jnp.where(not_last, pltpu.roll(here, NROW - 1, 1), 0.0)
            total += density_ref[start - 8 : start - 8 + STRIP]
            dst[start : start + STRIP] = total * share

    def two_sweeps(_, carry):
        sweep(even_ref, odd_ref)
        sweep(odd_ref, even_ref)
        return carry

    lax.fori_loop(0, (SWEEPS - 1) // 2, two_sweeps, 0)
    sweep(even_ref, odd_ref)
    weight = weight_ref[0]
    for tile in range(OWN // TILE):
        first = 8 + HALO + tile * TILE
        turned_ref[8 : 8 + NROW] = (odd_ref[first : first + TILE] * weight).T
        for band in range(BANDS):
            out_ref[band, tile * ROWS : (tile + 1) * ROWS] = turned_ref[
                R * band + 7 : R * band + 7 + ROWS
            ]


def relaxed(density, weight):
    return pl.pallas_call(
        relax_kernel,
        in_specs=[
            pl.BlockSpec(memory_space=pltpu.SMEM),
            pl.BlockSpec(memory_space=pltpu.VMEM),
        ],
        out_specs=pl.BlockSpec(memory_space=pltpu.VMEM),
        out_shape=jax.ShapeDtypeStruct((BANDS, MSG, TILE), jnp.float32),
        scratch_shapes=[
            pltpu.VMEM((SPAN + 16, NROW), jnp.float32),
            pltpu.VMEM((SPAN + 16, NROW), jnp.float32),
            pltpu.VMEM((NROW + 16, TILE), jnp.float32),
        ],
        compiler_params=pltpu.CompilerParams(vmem_limit_bytes=24 * 2**20),
        name="relaxed",
    )(weight, density)


GROUP = OWN // TILE


def chain_kernel(*refs):
    pieces, out_ref, held, sems = refs[:PLANES], refs[PLANES], refs[-2], refs[-1]
    me = lax.axis_index("plane")
    chip, core = me // 2, lax.rem(me, 2)
    order = []
    for back in range(4):
        for other in range(2):
            plane = 2 * lax.rem(chip - back + 4, 4) + (core + other * (1 - 2 * core))
            order.append(plane)
            copy = pltpu.make_async_copy(pieces[2 * back + other], held.at[plane], sems.at[plane])
            copy.start()
    for plane in range(PLANES):
        pltpu.make_async_copy(pieces[0], held.at[plane], sems.at[plane]).wait()
    lane = lax.broadcasted_iota(jnp.int32, (R, TILE), 1)
    is_first = lane == 0
    is_last = lane == TILE - 1

    def group_body(group, carry):
        here = pl.multiple_of(group * MSG, 8)
        behind = pl.multiple_of(lax.rem(group + BANDS - 1, BANDS) * MSG, 8)
        ahead = pl.multiple_of(lax.rem(group + 1, BANDS) * MSG, 8)
        starts = [behind + MSG - ROWS] + [here + t * ROWS for t in range(GROUP)] + [ahead]

        def plane_body(plane, state):
            mid, rise, both = [], [], []
            for start in starts:
                south = held[plane, pl.ds(start, R)]
                centre = held[plane, pl.ds(start + 1, R)]
                north = held[plane, pl.ds(start + 2, R)]
                mid.append(centre)
                rise.append(north - south)
                both.append(north + south)
            easts = [[pltpu.roll(x, TILE - 1, 1) for x in xs[1:]] for xs in (mid, rise)]
            wests = [[pltpu.roll(x, 1, 1) for x in xs[:-1]] for xs in (mid, rise)]
            new = []
            for t in range(GROUP):
                east, rise_east = (jnp.where(is_last, e[t + 1], e[t]) for e in easts)
                west, rise_west = (jnp.where(is_first, w[t], w[t + 1]) for w in wests)
                twice = 2.0 * mid[t + 1]
                c1 = 0.5 * (east - west)
                c2 = 0.5 * rise[t + 1]
                p11 = 1.0 - (east - twice + west)
                p22 = 1.0 - (both[t + 1] - twice)
                p12 = 0.25 * (rise_west - rise_east)
                a11, a12, a21, a22, s1, s2 = state[6 * t : 6 * t + 6]
                new += [
                    p11 * a11 + p12 * a21,
                    p11 * a12 + p12 * a22,
                    p12 * a11 + p22 * a21,
                    p12 * a12 + p22 * a22,
                    p11 * s1 + p12 * s2 + c1,
                    p12 * s1 + p22 * s2 + c2,
                ]
            return tuple(new)

        one = jnp.ones((R, TILE), jnp.float32)
        zero = jnp.zeros((R, TILE), jnp.float32)
        state = lax.fori_loop(0, me + 1, plane_body, (one, zero, zero, one, zero, zero) * GROUP)
        for t in range(GROUP):
            columns = pl.ds(pl.multiple_of(group * OWN + t * TILE, TILE), TILE)
            for entry in range(6):
                value = state[6 * t + entry]
                out_ref[0, entry, :, columns] = value - 1.0 if entry in (0, 3) else value
        return carry

    lax.fori_loop(0, BANDS, group_body, 0)


def chained(pieces):
    return pl.pallas_call(
        chain_kernel,
        in_specs=[pl.BlockSpec(memory_space=pl.ANY)] * PLANES,
        out_specs=pl.BlockSpec(memory_space=pltpu.VMEM),
        out_shape=jax.ShapeDtypeStruct((1, 6, R, NCOL), jnp.float32),
        scratch_shapes=[
            pltpu.VMEM((PLANES, BANDS * MSG, TILE), jnp.float32),
            pltpu.SemaphoreType.DMA((PLANES,)),
        ],
        compiler_params=pltpu.CompilerParams(vmem_limit_bytes=24 * 2**20),
        name="chained",
    )(*pieces)


def from_chip(block, back):
    return lax.ppermute(block, "plane", [(i, (i + 2 * back) % PLANES) for i in range(PLANES)])


def from_other_core(block):
    return lax.ppermute(block, "plane", [(i, i ^ 1) for i in range(PLANES)])


def body(slabs, slot_block, lens_weight):
    parts, scale = partial_densities(slabs[0], slot_block)
    sent = (parts * scale[0, 0]).astype(jnp.float16)
    got = lax.all_to_all(sent, "band", split_axis=0, concat_axis=0, tiled=True)
    unscale = jnp.exp2(got[:, 0:1, 0:1].astype(jnp.float32) - TOP)
    density = jnp.sum(got.astype(jnp.float32) * unscale, axis=0)
    messages = relaxed(density, lens_weight)
    rows = lax.all_to_all(messages, "band", split_axis=0, concat_axis=0, tiled=True)
    rows = rows.reshape(BANDS * MSG, TILE)
    chips = [rows] + [from_chip(rows, back) for back in (1, 2, 3)]
    pieces = []
    for piece in chips:
        pieces += [piece, from_other_core(piece)]
    return chained(pieces)


def solution(mesh):
    in_specs = (P("plane", "band", None, None), P("plane", "band"), P("plane"))
    out_specs = P("plane", None, "band", None)
    return jax.shard_map(body, mesh=mesh, in_specs=in_specs, out_specs=out_specs, check_vma=False)
```

```python
import functools

import jax
import jax.numpy as jnp
from jax import lax
from jax.experimental import pallas as pl
from jax.experimental.pallas import tpu as pltpu
from jax.sharding import PartitionSpec as P

NCOL = 8192
NROW = 128
R = 8
BLK = 4
SLOTS = 64
SWEEPS = 20
PLANES = 8
BANDS = 16
SIDE = 4
MASS = 0.05

OWN = NCOL // BANDS
HALO = 24
SPAN = OWN + 2 * HALO
TILE = 128
ROWS = R + 2
MSG = ROWS * OWN // TILE
TOP = 13.0
VMEM_BYTES = 54 * 2**20


ORDER = (2, 1, 3, 0)


def partial_kernel(slot_ref, slab_ref, *refs):
    out_refs, (power_ref, held, edges, select_ref, sems) = refs[:SIDE], refs[SIDE:]
    core = lax.rem(lax.axis_index("plane"), 2)
    me = lax.axis_index("band")
    my_y, my_z = me // SIDE, lax.rem(me, SIDE)

    def band_at(step, other):
        over_y = jnp.where(core == 0, other, step)
        over_z = jnp.where(core == 0, step, other)
        return SIDE * lax.rem(my_y + over_y, SIDE) + lax.rem(my_z + over_z, SIDE)

    def place(band):
        over_y = lax.rem(band // SIDE - my_y + SIDE, SIDE)
        over_z = lax.rem(lax.rem(band, SIDE) - my_z + SIDE, SIDE)
        return jnp.where(core == 0, SIDE * over_z + over_y, SIDE * over_y + over_z)

    def fetch(step, other):
        columns = pl.ds(pl.multiple_of(band_at(step, other) * OWN, OWN), OWN)
        index = SIDE * step + other
        return pltpu.make_async_copy(slab_ref.at[:, :, columns], held.at[index], sems.at[index])

    for step in ORDER:
        for other in range(SIDE):
            fetch(step, other).start()
    lane = lax.broadcasted_iota(jnp.int32, (8, NROW), 1)
    sub = lax.broadcasted_iota(jnp.int32, (8, NROW), 0)
    picks = []
    for pair in range(SLOTS // 2):
        block = jnp.where(sub < BLK, slot_ref[0, 2 * pair], slot_ref[0, 2 * pair + 1])
        row = block * BLK + (sub & (BLK - 1))
        picks.append(jnp.where(lane == row, 1.0, 0.0))
    select_ref[...] = jnp.concatenate(picks, 0).astype(jnp.bfloat16)

    most = jnp.zeros((8, NROW), jnp.float32)
    for step in ORDER:

        def chunk(other, most):
            fetch(step, other).wait()
            slabs = held[SIDE * step + other].reshape(SLOTS * BLK, OWN)
            part = lax.dot_general(
                slabs, select_ref[...], (((0,), (0,)), ((), ())), preferred_element_type=jnp.float32
            )
            out_refs[step][other, 0:OWN] = part
            band = band_at(step, other)
            edges[place(lax.rem(band + 1, BANDS)), 0:HALO] = part[OWN - HALO :]
            edges[place(lax.rem(band + BANDS - 1, BANDS)), HALO:] = part[:HALO]
            return jnp.maximum(most, jnp.max(jnp.abs(part).reshape(OWN // 8, 8, NROW), axis=0))

        most = lax.fori_loop(0, SIDE, chunk, most)
    for step in range(SIDE):
        for other in range(SIDE):
            out_refs[step][other, OWN:] = edges[SIDE * step + other]
    most = jnp.full((8, NROW), jnp.max(most), jnp.float32)
    power_ref[...] = jnp.ceil(jnp.log2(jnp.maximum(most, 2.0**-100)))[0:1]


def partial_densities(slabs, slot_block):
    part = pltpu.VMEM((SIDE, SPAN, NROW), jnp.float32)
    return pl.pallas_call(
        partial_kernel,
        in_specs=[pl.BlockSpec(memory_space=pltpu.SMEM), pl.BlockSpec(memory_space=pl.ANY)],
        out_specs=[pl.BlockSpec(memory_space=pltpu.VMEM)] * (SIDE + 1),
        out_shape=[part] * SIDE + [jax.ShapeDtypeStruct((1, NROW), jnp.float32)],
        scratch_shapes=[
            pltpu.VMEM((BANDS, SLOTS, BLK, OWN), jnp.bfloat16),
            pltpu.VMEM((BANDS, 2 * HALO, NROW), jnp.float32),
            pltpu.VMEM((SLOTS * BLK, NROW), jnp.bfloat16),
            pltpu.SemaphoreType.DMA((BANDS,)),
        ],
        compiler_params=pltpu.CompilerParams(vmem_limit_bytes=VMEM_BYTES),
        name="partial_densities",
    )(slot_block, slabs)


STRIP = 80


def relax_kernel(weight_ref, part_ref, out_ref, density_ref, even_ref, odd_ref, turned_ref):
    zero = jnp.zeros((8, NROW), jnp.float32)
    for ref in (even_ref, odd_ref):
        ref[0:8] = zero
        ref[8 + SPAN :] = zero
    turned_ref[0:8] = zero
    turned_ref[8 + NROW :] = zero
    lane = lax.broadcasted_iota(jnp.int32, (STRIP, NROW), 1)
    not_first = lane > 0
    not_last = lane < NROW - 1
    share = 1.0 / (4.0 + MASS)

    def begin(start, block):
        density_ref[start : start + block.shape[0]] = block
        even_ref[8 + start : 8 + start + block.shape[0]] = block * share

    begin(0, part_ref[OWN : OWN + HALO])
    begin(HALO + OWN, part_ref[OWN + HALO :])
    for tile in range(OWN // TILE):
        begin(HALO + tile * TILE, part_ref[tile * TILE : (tile + 1) * TILE])

    def sweep(src, dst):
        for start in range(8, 8 + SPAN, STRIP):
            here = src[start : start + STRIP]
            total = src[start - 1 : start - 1 + STRIP] + src[start + 1 : start + 1 + STRIP]
            total += jnp.where(not_first, pltpu.roll(here, 1, 1), 0.0)
            total += jnp.where(not_last, pltpu.roll(here, NROW - 1, 1), 0.0)
            total += density_ref[start - 8 : start - 8 + STRIP]
            dst[start : start + STRIP] = total * share

    def two_sweeps(_, carry):
        sweep(even_ref, odd_ref)
        sweep(odd_ref, even_ref)
        return carry

    lax.fori_loop(0, (SWEEPS - 1) // 2, two_sweeps, 0)
    sweep(even_ref, odd_ref)
    weight = weight_ref[0]
    for tile in range(OWN // TILE):
        first = 8 + HALO + tile * TILE
        turned_ref[8 : 8 + NROW] = (odd_ref[first : first + TILE] * weight).T
        for band in range(BANDS):
            out_ref[BANDS - 1 - band, tile * ROWS : (tile + 1) * ROWS] = turned_ref[
                R * band + 7 : R * band + 7 + ROWS
            ]


def relaxed(density, weight):
    return pl.pallas_call(
        relax_kernel,
        in_specs=[
            pl.BlockSpec(memory_space=pltpu.SMEM),
            pl.BlockSpec(memory_space=pltpu.VMEM),
        ],
        out_specs=pl.BlockSpec(memory_space=pltpu.VMEM),
        out_shape=jax.ShapeDtypeStruct((BANDS, MSG, TILE), jnp.float32),
        scratch_shapes=[
            pltpu.VMEM((SPAN, NROW), jnp.float32),
            pltpu.VMEM((SPAN + 16, NROW), jnp.float32),
            pltpu.VMEM((SPAN + 16, NROW), jnp.float32),
            pltpu.VMEM((NROW + 16, TILE), jnp.float32),
        ],
        compiler_params=pltpu.CompilerParams(vmem_limit_bytes=24 * 2**20),
        name="relaxed",
    )(weight, density)


GROUP = OWN // TILE


def plane_maps(ref, starts, is_first, is_last):
    mid, rise, both = [], [], []
    for start in starts:
        south, north = ref[pl.ds(start, R)], ref[pl.ds(start + 2, R)]
        mid.append(ref[pl.ds(start + 1, R)])
        rise.append(north - south)
        both.append(north + south)
    easts = [[pltpu.roll(x, TILE - 1, 1) for x in xs[1:]] for xs in (mid, rise)]
    wests = [[pltpu.roll(x, 1, 1) for x in xs[:-1]] for xs in (mid, rise)]
    maps = []
    for t in range(GROUP):
        east, rise_east = (jnp.where(is_last, e[t + 1], e[t]) for e in easts)
        west, rise_west = (jnp.where(is_first, w[t], w[t + 1]) for w in wests)
        twice = 2.0 * mid[t + 1]
        p11 = 1.0 - (east - twice + west)
        p22 = 1.0 - (both[t + 1] - twice)
        p12 = 0.25 * (rise_west - rise_east)
        maps.append((p11, p12, p22, 0.5 * (east - west), 0.5 * rise[t + 1]))
    return maps


def after_map(state, maps):
    a11, a12, a21, a22, s1, s2 = state
    p11, p12, p22, c1, c2 = maps
    return (
        a11 * p11 + a12 * p12,
        a11 * p12 + a12 * p22,
        a21 * p11 + a22 * p12,
        a21 * p12 + a22 * p22,
        a11 * c1 + a12 * c2 + s1,
        a21 * c1 + a22 * c2 + s2,
    )


def after_state(state, first):
    a11, a12, a21, a22, s1, s2 = state
    b11, b12, b21, b22, t1, t2 = first
    return (
        a11 * b11 + a12 * b21,
        a11 * b12 + a12 * b22,
        a21 * b11 + a22 * b21,
        a21 * b12 + a22 * b22,
        a11 * t1 + a12 * t2 + s1,
        a21 * t1 + a22 * t2 + s2,
    )


def chain_step(state_ref, out_ref, pieces, first_ref=None, last=False):
    lane = lax.broadcasted_iota(jnp.int32, (R, TILE), 1)
    is_first = lane == 0
    is_last = lane == TILE - 1

    def group_body(group, carry):
        here = pl.multiple_of(group * MSG, 8)
        behind = pl.multiple_of(lax.rem(group + 1, BANDS) * MSG, 8)
        ahead = pl.multiple_of(lax.rem(group + BANDS - 1, BANDS) * MSG, 8)
        starts = [behind + MSG - ROWS] + [here + t * ROWS for t in range(GROUP)] + [ahead]
        first = (BANDS - 1 - group) * OWN
        columns = [pl.ds(pl.multiple_of(first + t * TILE, TILE), TILE) for t in range(GROUP)]
        maps = [plane_maps(piece, starts, is_first, is_last) for piece in pieces]
        for t in range(GROUP):
            if state_ref is None:
                p11, p12, p22, c1, c2 = maps[0][t]
                state = (p11, p12, p12, p22, c1, c2)
                rest = maps[1:]
            else:
                state = tuple(state_ref[entry, :, columns[t]] for entry in range(6))
                rest = maps
            for one in rest:
                state = after_map(state, one[t])
            if first_ref is not None:
                state = after_state(state, [first_ref[entry, :, columns[t]] for entry in range(6)])
            if last:
                state = tuple(x - 1.0 if e in (0, 3) else x for e, x in enumerate(state))
            for entry in range(6):
                out_ref[entry, :, columns[t]] = state[entry]
        return carry

    lax.fori_loop(0, BANDS, group_body, 0)


def recent_kernel(back, own_ref, other_ref, one_ref, one_other_ref, out_ref):
    me = lax.axis_index("plane")
    chip, core = me // 2, lax.rem(me, 2)
    for which in (0, 1):
        near = [own_ref, other_ref] if which else [own_ref]
        far = [one_ref, one_other_ref] if which else [one_other_ref, one_ref]

        @pl.when(jnp.logical_and(chip < back, core == which))
        def _():
            chain_step(None, out_ref, near)

        @pl.when(jnp.logical_and(chip >= back, core == which))
        def _():
            chain_step(None, out_ref, near + far)


def first_kernel(back, own_ref, other_ref, out_ref):
    me = lax.axis_index("plane")
    chip, core = me // 2, lax.rem(me, 2)
    for which in (0, 1):
        pieces = [own_ref, other_ref] if which else [other_ref, own_ref]

        @pl.when(jnp.logical_and(chip >= back, core == which))
        def _():
            chain_step(None, out_ref, pieces)


def finish_kernel(back, state_ref, own_ref, other_ref, first_ref, out_ref):
    me = lax.axis_index("plane")
    chip, core = me // 2, lax.rem(me, 2)
    out_ref = out_ref.at[0]

    @pl.when(chip < back)
    def _():
        chain_step(state_ref, out_ref, [], last=True)

    for which in (0, 1):
        pieces = [own_ref, other_ref] if which else [other_ref, own_ref]

        @pl.when(jnp.logical_and(chip == back, core == which))
        def _():
            chain_step(state_ref, out_ref, pieces, last=True)

        @pl.when(jnp.logical_and(chip > back, core == which))
        def _():
            chain_step(state_ref, out_ref, pieces, first_ref, last=True)


def chain_call(kernel, name, operands, shape):
    vmem = pl.BlockSpec(memory_space=pltpu.VMEM)
    return pl.pallas_call(
        kernel,
        in_specs=[vmem] * len(operands),
        out_specs=vmem,
        out_shape=jax.ShapeDtypeStruct(shape, jnp.float32),
        cost_estimate=pl.CostEstimate(
            flops=80 * R * NCOL,
            bytes_accessed=sum(4 * x.size for x in operands) + 24 * R * NCOL,
            transcendentals=0,
        ),
        compiler_params=pltpu.CompilerParams(vmem_limit_bytes=16 * 2**20),
        name=name,
    )(*operands)


def from_chip(block, back):
    return lax.ppermute(block, "plane", [(i, (i + 2 * back) % PLANES) for i in range(PLANES)])


def from_other_core(block):
    return lax.ppermute(block, "plane", [(i, i ^ 1) for i in range(PLANES)])


def along_band(block, steps, first):
    route = []
    for plane in range(PLANES):
        for y in range(SIDE):
            for z in range(SIDE):
                if (plane % 2 == 0) == first:
                    target = SIDE * y + (z + steps) % SIDE
                else:
                    target = SIDE * ((y + steps) % SIDE) + z
                route.append((plane * BANDS + SIDE * y + z, plane * BANDS + target))
    return lax.ppermute(block, ("plane", "band"), route)


def coded(values, power):
    row = lax.broadcasted_iota(jnp.int32, values.shape, values.ndim - 2)
    scaled = values * jnp.exp2(TOP - power)
    return jnp.where(row == OWN, power, scaled).astype(jnp.float16)


def power_of(code):
    return code.reshape(-1, SPAN, NROW)[0, OWN : OWN + 1].astype(jnp.float32)


def decoded(code, factor):
    return code.astype(jnp.float32) * factor


def reduced_density(slabs, slot_block):
    *parts, power = partial_densities(slabs, slot_block)
    codes = {}
    for step, after in ((2, 1), (1, 3), (3, 0)):
        code = coded(parts[step], power)
        code, parts[after] = lax.optimization_barrier((code, parts[after]))
        codes[step] = along_band(code, step, True)
    powers = [power_of(codes[step]) for step in (1, 2, 3)]
    power = functools.reduce(jnp.maximum, powers, power)
    factors = [jnp.exp2(power - TOP) for power in powers]
    sums = {}
    for other in (2, 1, 3, 0):
        total = parts[0][other]
        for step in (1, 2, 3):
            total += decoded(codes[step][other], factors[step - 1])
        sums[other] = total if other == 0 else along_band(coded(total, power), other, False)
    for other in (1, 2, 3):
        total = sums[0]
        factor = jnp.exp2(power_of(sums[other]) - TOP)
        sums[0] = total + decoded(sums[other], factor)
    return sums[0]


def body(slabs, slot_block, lens_weight):
    density = reduced_density(slabs[0], slot_block)
    messages = relaxed(density, lens_weight)
    backwards = [list(range(BANDS))[::-1]]
    rows = lax.all_to_all(
        messages, "band", split_axis=0, concat_axis=0, axis_index_groups=backwards, tiled=True
    )
    rows = rows.reshape(BANDS * MSG, TILE)
    two, one, three = (from_chip(rows, back) for back in (2, 1, 3))
    shape = (6, R, NCOL)
    recent = functools.partial(recent_kernel, 1)
    operands = (rows, from_other_core(rows), one, from_other_core(one))
    recent = chain_call(recent, "chain_recent", operands, shape)
    first = functools.partial(first_kernel, 3)
    first = chain_call(first, "chain_first", (three, from_other_core(three)), shape)
    finish = functools.partial(finish_kernel, 2)
    operands = (recent, two, from_other_core(two), first)
    return chain_call(finish, "chain_finish", operands, (1,) + shape)


def solution(mesh):
    in_specs = (P("plane", "band", None, None), P("plane", "band"), P("plane"))
    out_specs = P("plane", None, "band", None)
    return jax.shard_map(body, mesh=mesh, in_specs=in_specs, out_specs=out_specs, check_vma=False)
```

```python
import functools

import jax
import jax.numpy as jnp
from jax import lax
from jax.experimental import pallas as pl
from jax.experimental.pallas import tpu as pltpu
from jax.sharding import PartitionSpec as P

NCOL = 8192
NROW = 128
R = 8
BLK = 4
SLOTS = 64
SWEEPS = 20
PLANES = 8
BANDS = 16
SIDE = 4
MASS = 0.05

OWN = NCOL // BANDS
HALO = 24
SPAN = OWN + 2 * HALO
TILE = 128
ROWS = R + 2
MSG = ROWS * OWN // TILE
TOP = 13.0
VMEM_BYTES = 54 * 2**20


FAR, NEAR = 2, (1, 3, 0)
ORDER = (1, 3, 2, 0)


class Relay:
    def __init__(self):
        self.core = lax.rem(lax.axis_index("plane"), 2)
        self.me = lax.axis_index("band")

    def band_at(self, step, other):
        over_y = jnp.where(self.core == 0, other, step)
        over_z = jnp.where(self.core == 0, step, other)
        return self.me ^ (SIDE * over_y + over_z)

    def place(self, band):
        over_y, over_z = (self.me ^ band) // SIDE, (self.me ^ band) % SIDE
        return jnp.where(self.core == 0, SIDE * over_z + over_y, SIDE * over_y + over_z)


def before(band):
    return lax.rem(band + BANDS - 1, BANDS)


def after(band):
    return lax.rem(band + 1, BANDS)


def fill_select(slot_ref, select_ref, turned_ref):
    lane = lax.broadcasted_iota(jnp.int32, (8, NROW), 1)
    sub = lax.broadcasted_iota(jnp.int32, (8, NROW), 0)
    picks = []
    for pair in range(SLOTS // 2):
        block = jnp.where(sub < BLK, slot_ref[0, 2 * pair], slot_ref[0, 2 * pair + 1])
        row = block * BLK + (sub & (BLK - 1))
        picks.append(jnp.where(lane == row, 1.0, 0.0))
    select = jnp.concatenate(picks, 0)
    select_ref[...] = select.astype(jnp.bfloat16)
    turned_ref[...] = select.T.astype(jnp.bfloat16)


def summed_turned(slabs, select_ref):
    return lax.dot_general(
        slabs, select_ref[...], (((0,), (0,)), ((), ())), preferred_element_type=jnp.float32
    )


def summed(slabs, turned_ref):
    return jnp.dot(turned_ref[...], slabs, preferred_element_type=jnp.float32)


def larger(most, part):
    return jnp.maximum(most, jnp.max(jnp.abs(part).reshape(-1, 8, NROW), axis=0))


def outer_tiles(slabs):
    return jnp.concatenate([slabs[:, :TILE], slabs[:, -TILE:]], axis=1)


def store_part(out_ref, other, slabs, select_ref, turned_ref, most):
    outer = summed_turned(outer_tiles(slabs), select_ref)
    out_ref[other, 0:TILE] = outer[:TILE]
    out_ref[other, OWN - TILE : OWN] = outer[TILE:]
    inner = summed(slabs[:, TILE : OWN - TILE], turned_ref)
    for tile in range(1, OWN // TILE - 1):
        part = inner[:, (tile - 1) * TILE : tile * TILE]
        out_ref[other, tile * TILE : (tile + 1) * TILE] = part
        most = larger(most, part)
    return outer[:HALO], outer[2 * TILE - HALO :], larger(most, outer)


def power_above(most):
    most = jnp.full((8, NROW), jnp.max(most), jnp.float32)
    return jnp.ceil(jnp.log2(jnp.maximum(most, 2.0**-100)))[0:1]


def far_kernel(slot_ref, slab_ref, out_ref, edges_ref, power_ref, held, select_ref, turned_ref, sems):
    relay = Relay()

    def fetches(other):
        band = relay.band_at(FAR, other)
        pieces = [
            (before(band) * OWN + OWN - TILE, TILE, 0),
            (band * OWN, OWN, TILE),
            (after(band) * OWN, TILE, TILE + OWN),
        ]
        return [
            pltpu.make_async_copy(
                slab_ref.at[:, :, pl.ds(pl.multiple_of(first, TILE), width)],
                held.at[other, :, :, pl.ds(to, width)],
                sems.at[other, piece],
            )
            for piece, (first, width, to) in enumerate(pieces)
        ]

    for other in range(SIDE):
        for copy in fetches(other):
            copy.start()
    fill_select(slot_ref, select_ref, turned_ref)

    def chunk(other, most):
        for copy in fetches(other):
            copy.wait()
        band = relay.band_at(FAR, other)
        slabs = held[other].reshape(SLOTS * BLK, OWN + 2 * TILE)
        low, high, most = store_part(
            out_ref, other, slabs[:, TILE : TILE + OWN], select_ref, turned_ref, most
        )
        edges_ref[relay.place(after(band)), 0:HALO] = high
        edges_ref[relay.place(before(band)), HALO:] = low
        outer = summed_turned(outer_tiles(slabs), select_ref)
        left, right = outer[TILE - HALO : TILE], outer[TILE : TILE + HALO]
        out_ref[other, OWN : OWN + HALO] = left
        out_ref[other, OWN + HALO :] = right
        return larger(larger(most, left), right)

    most = lax.fori_loop(0, SIDE, chunk, jnp.zeros((8, NROW), jnp.float32))
    power_ref[...] = power_above(most)


def near_kernel(slot_ref, slab_ref, far_edges_ref, *refs):
    out_refs, refs = refs[: len(NEAR)], refs[len(NEAR) :]
    power_ref, held, edges, select_ref, turned_ref, sems = refs
    relay = Relay()

    def band_of(slot):
        step = jnp.where(slot < SIDE, NEAR[0], jnp.where(slot < 2 * SIDE, NEAR[1], NEAR[2]))
        return relay.band_at(step, lax.rem(slot, SIDE))

    def fetch(slot):
        columns = pl.ds(pl.multiple_of(band_of(slot) * OWN, OWN), OWN)
        return pltpu.make_async_copy(slab_ref.at[:, :, columns], held.at[slot], sems.at[slot])

    for slot in range(len(NEAR) * SIDE):
        fetch(slot).start()
    fill_select(slot_ref, select_ref, turned_ref)
    edges[...] = far_edges_ref[...]

    def chunks(index, most):
        def chunk(other, most):
            slot = SIDE * index + other
            fetch(slot).wait()
            slabs = held[slot].reshape(SLOTS * BLK, OWN)
            low, high, most = store_part(
                out_refs[index], other, slabs, select_ref, turned_ref, most
            )
            edges[relay.place(after(band_of(slot))), 0:HALO] = high
            edges[relay.place(before(band_of(slot))), HALO:] = low
            return most

        return lax.fori_loop(0, SIDE, chunk, most)

    most = jnp.zeros((8, NROW), jnp.float32)
    for index in range(len(NEAR)):
        most = chunks(index, most)
    for index, step in enumerate(NEAR):
        for other in range(SIDE):
            block = edges[SIDE * step + other]
            out_refs[index][other, OWN:] = block
            most = larger(most, block)
    power_ref[...] = power_above(most)


def sum_call(kernel, name, operands, parts, more, held, sems):
    vmem = pl.BlockSpec(memory_space=pltpu.VMEM)
    return pl.pallas_call(
        kernel,
        in_specs=[pl.BlockSpec(memory_space=pltpu.SMEM), pl.BlockSpec(memory_space=pl.ANY)]
        + [vmem] * (len(operands) - 2),
        out_specs=[vmem] * (parts + len(more)),
        out_shape=[pltpu.VMEM((SIDE, SPAN, NROW), jnp.float32)] * parts + more,
        scratch_shapes=held
        + [
            pltpu.VMEM((SLOTS * BLK, NROW), jnp.bfloat16),
            pltpu.VMEM((NROW, SLOTS * BLK), jnp.bfloat16),
            pltpu.SemaphoreType.DMA(sems),
        ],
        compiler_params=pltpu.CompilerParams(vmem_limit_bytes=VMEM_BYTES),
        name=name,
    )(*operands)


POWER = pltpu.VMEM((1, NROW), jnp.float32)
EDGES = pltpu.VMEM((BANDS, 2 * HALO, NROW), jnp.float32)


def far_sums(slabs, slot_block):
    held = pltpu.VMEM((SIDE, SLOTS, BLK, OWN + 2 * TILE), jnp.bfloat16)
    operands = (slot_block, slabs)
    return sum_call(far_kernel, "far_sums", operands, 1, [EDGES, POWER], [held], (SIDE, 3))


def near_sums(slabs, slot_block, edges):
    count = SIDE * len(NEAR)
    held = pltpu.VMEM((count, SLOTS, BLK, OWN), jnp.bfloat16)
    operands = (slot_block, slabs, edges)
    return sum_call(near_kernel, "near_sums", operands, 3, [POWER], [held, EDGES], (count,))


STEPS = SPAN // 8


def relax_kernel(weight_ref, part_ref, out_ref, plain_ref, density_ref, even_ref, odd_ref, turned_ref):
    zero = jnp.zeros((8, NROW), jnp.float32)
    turned_ref[0:8] = zero
    turned_ref[8 + NROW :] = zero
    lane = lax.broadcasted_iota(jnp.int32, (8, NROW), 1)
    not_first = lane > 0
    not_last = lane < NROW - 1
    share = 1.0 / (4.0 + MASS)

    plain_ref[0:HALO] = part_ref[OWN : OWN + HALO]
    plain_ref[HALO + OWN :] = part_ref[OWN + HALO :]
    for tile in range(OWN // TILE):
        part = part_ref[tile * TILE : (tile + 1) * TILE]
        part = part if tile in (0, OWN // TILE - 1) else part.T
        plain_ref[HALO + tile * TILE : HALO + (tile + 1) * TILE] = part

    for t in range(STEPS):
        block = plain_ref[pl.ds(t, 8, stride=STEPS)]
        density_ref[8 * t : 8 * t + 8] = block
        even_ref[8 * t : 8 * t + 8] = block * share

    def sweep(src, dst):
        first = here = src[0:8]
        behind = pltpu.roll(src[8 * STEPS - 8 :], 1, 0)
        for t in range(STEPS):
            ahead = src[8 * t + 8 : 8 * t + 16] if t < STEPS - 1 else pltpu.roll(first, 7, 0)
            total = behind + ahead + density_ref[8 * t : 8 * t + 8]
            total += jnp.where(not_first, pltpu.roll(here, 1, 1), 0.0)
            total += jnp.where(not_last, pltpu.roll(here, NROW - 1, 1), 0.0)
            dst[8 * t : 8 * t + 8] = total * share
            behind, here = here, ahead

    def two_sweeps(_, carry):
        sweep(even_ref, odd_ref)
        sweep(odd_ref, even_ref)
        return carry

    lax.fori_loop(0, (SWEEPS - 1) // 2, two_sweeps, 0)
    sweep(even_ref, odd_ref)
    weight = weight_ref[0]
    for t in range(STEPS):
        plain_ref[pl.ds(t, 8, stride=STEPS)] = odd_ref[8 * t : 8 * t + 8] * weight
    for tile in range(OWN // TILE):
        first = HALO + tile * TILE
        turned_ref[8 : 8 + NROW] = plain_ref[first : first + TILE].T
        for band in range(BANDS):
            out_ref[BANDS - 1 - band, tile * ROWS : (tile + 1) * ROWS] = turned_ref[
                R * band + 7 : R * band + 7 + ROWS
            ]


def relaxed(density, weight):
    return pl.pallas_call(
        relax_kernel,
        in_specs=[
            pl.BlockSpec(memory_space=pltpu.SMEM),
            pl.BlockSpec(memory_space=pltpu.VMEM),
        ],
        out_specs=pl.BlockSpec(memory_space=pltpu.VMEM),
        out_shape=jax.ShapeDtypeStruct((BANDS, MSG, TILE), jnp.float32),
        scratch_shapes=[
            pltpu.VMEM((SPAN, NROW), jnp.float32),
            pltpu.VMEM((SPAN, NROW), jnp.float32),
            pltpu.VMEM((SPAN, NROW), jnp.float32),
            pltpu.VMEM((SPAN, NROW), jnp.float32),
            pltpu.VMEM((NROW + 16, TILE), jnp.float32),
        ],
        compiler_params=pltpu.CompilerParams(vmem_limit_bytes=24 * 2**20),
        name="relaxed",
    )(weight, density)


GROUP = OWN // TILE


def plane_maps(ref, starts, is_first, is_last):
    mid, rise, both = [], [], []
    for start in starts:
        south, north = ref[pl.ds(start, R)], ref[pl.ds(start + 2, R)]
        mid.append(ref[pl.ds(start + 1, R)])
        rise.append(north - south)
        both.append(north + south)
    easts = [[pltpu.roll(x, TILE - 1, 1) for x in xs[1:]] for xs in (mid, rise)]
    wests = [[pltpu.roll(x, 1, 1) for x in xs[:-1]] for xs in (mid, rise)]
    maps = []
    for t in range(GROUP):
        east, rise_east = (jnp.where(is_last, e[t + 1], e[t]) for e in easts)
        west, rise_west = (jnp.where(is_first, w[t], w[t + 1]) for w in wests)
        twice = 2.0 * mid[t + 1]
        p11 = 1.0 - (east - twice + west)
        p22 = 1.0 - (both[t + 1] - twice)
        p12 = 0.25 * (rise_west - rise_east)
        maps.append((p11, p12, p22, 0.5 * (east - west), 0.5 * rise[t + 1]))
    return maps


def after_map(state, maps):
    a11, a12, a21, a22, s1, s2 = state
    p11, p12, p22, c1, c2 = maps
    return (
        a11 * p11 + a12 * p12,
        a11 * p12 + a12 * p22,
        a21 * p11 + a22 * p12,
        a21 * p12 + a22 * p22,
        a11 * c1 + a12 * c2 + s1,
        a21 * c1 + a22 * c2 + s2,
    )


def after_state(state, first):
    a11, a12, a21, a22, s1, s2 = state
    b11, b12, b21, b22, t1, t2 = first
    return (
        a11 * b11 + a12 * b21,
        a11 * b12 + a12 * b22,
        a21 * b11 + a22 * b21,
        a21 * b12 + a22 * b22,
        a11 * t1 + a12 * t2 + s1,
        a21 * t1 + a22 * t2 + s2,
    )


def chain_step(state_ref, out_ref, pieces, first_ref=None, last=False):
    lane = lax.broadcasted_iota(jnp.int32, (R, TILE), 1)
    is_first = lane == 0
    is_last = lane == TILE - 1

    def group_body(group, carry):
        here = pl.multiple_of(group * MSG, 8)
        behind = pl.multiple_of(lax.rem(group + 1, BANDS) * MSG, 8)
        ahead = pl.multiple_of(lax.rem(group + BANDS - 1, BANDS) * MSG, 8)
        starts = [behind + MSG - ROWS] + [here + t * ROWS for t in range(GROUP)] + [ahead]
        first = (BANDS - 1 - group) * OWN
        columns = [pl.ds(pl.multiple_of(first + t * TILE, TILE), TILE) for t in range(GROUP)]
        maps = [plane_maps(piece, starts, is_first, is_last) for piece in pieces]
        for t in range(GROUP):
            if state_ref is None:
                p11, p12, p22, c1, c2 = maps[0][t]
                state = (p11, p12, p12, p22, c1, c2)
                rest = maps[1:]
            else:
                state = tuple(state_ref[entry, :, columns[t]] for entry in range(6))
                rest = maps
            for one in rest:
                state = after_map(state, one[t])
            if first_ref is not None:
                state = after_state(state, [first_ref[entry, :, columns[t]] for entry in range(6)])
            if last:
                state = tuple(x - 1.0 if e in (0, 3) else x for e, x in enumerate(state))
            for entry in range(6):
                out_ref[entry, :, columns[t]] = state[entry]
        return carry

    lax.fori_loop(0, BANDS, group_body, 0, unroll=4)


def recent_kernel(back, own_ref, other_ref, one_ref, one_other_ref, out_ref):
    me = lax.axis_index("plane")
    chip, core = me // 2, lax.rem(me, 2)
    for which in (0, 1):
        near = [own_ref, other_ref] if which else [own_ref]
        far = [one_ref, one_other_ref] if which else [one_other_ref, one_ref]

        @pl.when(jnp.logical_and(chip < back, core == which))
        def _():
            chain_step(None, out_ref, near)

        @pl.when(jnp.logical_and(chip >= back, core == which))
        def _():
            chain_step(None, out_ref, near + far)


def first_kernel(back, own_ref, other_ref, out_ref):
    me = lax.axis_index("plane")
    chip, core = me // 2, lax.rem(me, 2)
    for which in (0, 1):
        pieces = [own_ref, other_ref] if which else [other_ref, own_ref]

        @pl.when(jnp.logical_and(chip >= back, core == which))
        def _():
            chain_step(None, out_ref, pieces)


def finish_kernel(back, state_ref, own_ref, other_ref, first_ref, out_ref):
    me = lax.axis_index("plane")
    chip, core = me // 2, lax.rem(me, 2)
    out_ref = out_ref.at[0]

    @pl.when(chip < back)
    def _():
        chain_step(state_ref, out_ref, [], last=True)

    for which in (0, 1):
        pieces = [own_ref, other_ref] if which else [other_ref, own_ref]

        @pl.when(jnp.logical_and(chip == back, core == which))
        def _():
            chain_step(state_ref, out_ref, pieces, last=True)

        @pl.when(jnp.logical_and(chip > back, core == which))
        def _():
            chain_step(state_ref, out_ref, pieces, first_ref, last=True)


def chain_call(kernel, name, operands, shape):
    vmem = pl.BlockSpec(memory_space=pltpu.VMEM)
    return pl.pallas_call(
        kernel,
        in_specs=[vmem] * len(operands),
        out_specs=vmem,
        out_shape=jax.ShapeDtypeStruct(shape, jnp.float32),
        cost_estimate=pl.CostEstimate(
            flops=80 * R * NCOL,
            bytes_accessed=sum(4 * x.size for x in operands) + 24 * R * NCOL,
            transcendentals=0,
        ),
        compiler_params=pltpu.CompilerParams(vmem_limit_bytes=16 * 2**20),
        name=name,
    )(*operands)


def from_chip(block, back):
    return lax.ppermute(block, "plane", [(i, (i + 2 * back) % PLANES) for i in range(PLANES)])


def from_other_core(block):
    return lax.ppermute(block, "plane", [(i, i ^ 1) for i in range(PLANES)])


def exchanged(block, step, first):
    route = []
    for plane in range(PLANES):
        side = 1 if (plane % 2 == 0) == first else SIDE
        for band in range(BANDS):
            route.append((plane * BANDS + band, plane * BANDS + (band ^ (step * side))))
    return lax.ppermute(block, ("plane", "band"), route)


def coded(values, power):
    row = lax.broadcasted_iota(jnp.int32, values.shape, values.ndim - 2)
    scaled = values * jnp.exp2(TOP - power)
    return jnp.where(row == OWN, power, scaled).astype(jnp.float16)


def power_of(code):
    return code.reshape(-1, SPAN, NROW)[0, OWN : OWN + 1].astype(jnp.float32)


def decoded(code, factor):
    return code.astype(jnp.float32) * factor


def reduced_density(slabs, slot_block):
    far, edges, power = far_sums(slabs, slot_block)
    code = coded(far, power)
    code, edges = lax.optimization_barrier((code, edges))
    codes = {FAR: exchanged(code, FAR, True)}
    *parts, power = near_sums(slabs, slot_block, edges)
    parts = dict(zip(NEAR, parts))
    for step in NEAR[:2]:
        codes[step] = exchanged(coded(parts[step], power), step, True)
    powers = [power_of(codes[step]) for step in ORDER[:3]]
    power = functools.reduce(jnp.maximum, powers, power)
    factors = {step: jnp.exp2(x - TOP) for step, x in zip(ORDER, powers)}
    sums = {}
    for other in ORDER:
        total = parts[0][other]
        for step in ORDER[:3]:
            total += decoded(codes[step][other], factors[step])
        sums[other] = total if other == 0 else exchanged(coded(total, power), other, False)
    for other in ORDER[:3]:
        total = sums[0]
        factor = jnp.exp2(power_of(sums[other]) - TOP)
        sums[0] = total + decoded(sums[other], factor)
    return sums[0]


def body(slabs, slot_block, lens_weight):
    density = reduced_density(slabs[0], slot_block)
    messages = relaxed(density, lens_weight)
    backwards = [list(range(BANDS))[::-1]]
    rows = lax.all_to_all(
        messages, "band", split_axis=0, concat_axis=0, axis_index_groups=backwards, tiled=True
    )
    rows = rows.reshape(BANDS * MSG, TILE)
    two, one, three = (from_chip(rows, back) for back in (2, 1, 3))
    shape = (6, R, NCOL)
    recent = functools.partial(recent_kernel, 1)
    operands = (rows, from_other_core(rows), one, from_other_core(one))
    recent = chain_call(recent, "chain_recent", operands, shape)
    first = functools.partial(first_kernel, 3)
    first = chain_call(first, "chain_first", (three, from_other_core(three)), shape)
    finish = functools.partial(finish_kernel, 2)
    operands = (recent, two, from_other_core(two), first)
    return chain_call(finish, "chain_finish", operands, (1,) + shape)


def solution(mesh):
    in_specs = (P("plane", "band", None, None), P("plane", "band"), P("plane"))
    out_specs = P("plane", None, "band", None)
    return jax.shard_map(body, mesh=mesh, in_specs=in_specs, out_specs=out_specs, check_vma=False)
```

```python
import functools

import jax
import jax.numpy as jnp
from jax import lax
from jax.experimental import pallas as pl
from jax.experimental.pallas import tpu as pltpu
from jax.sharding import PartitionSpec as P

NCOL = 8192
NROW = 128
R = 8
BLK = 4
SLOTS = 64
SWEEPS = 20
PLANES = 8
BANDS = 16
SIDE = 4
MASS = 0.05

OWN = NCOL // BANDS
HALO = 24
SPAN = OWN + 2 * HALO
TILE = 128
ROWS = R + 2
MSG = ROWS * OWN // TILE
TOP = 13.0
VMEM_BYTES = 53 * 2**20


FAR, NEAR = 2, (1, 3, 0)
ORDER = (1, 3, 2, 0)


class Relay:
    def __init__(self):
        self.core = lax.rem(lax.axis_index("plane"), 2)
        self.me = lax.axis_index("band")

    def band_at(self, step, other):
        over_y = jnp.where(self.core == 0, other, step)
        over_z = jnp.where(self.core == 0, step, other)
        return self.me ^ (SIDE * over_y + over_z)

    def place(self, band):
        over_y, over_z = (self.me ^ band) // SIDE, (self.me ^ band) % SIDE
        return jnp.where(self.core == 0, SIDE * over_z + over_y, SIDE * over_y + over_z)


def before(band):
    return lax.rem(band + BANDS - 1, BANDS)


def after(band):
    return lax.rem(band + 1, BANDS)


def fill_select(slot_ref, select_ref, turned_ref):
    lane = lax.broadcasted_iota(jnp.int32, (8, NROW), 1)
    sub = lax.broadcasted_iota(jnp.int32, (8, NROW), 0)
    picks = []
    for pair in range(SLOTS // 2):
        block = jnp.where(sub < BLK, slot_ref[0, 2 * pair], slot_ref[0, 2 * pair + 1])
        row = block * BLK + (sub & (BLK - 1))
        picks.append(jnp.where(lane == row, 1.0, 0.0))
    select = jnp.concatenate(picks, 0)
    select_ref[...] = select.astype(jnp.bfloat16)
    turned_ref[...] = select.T.astype(jnp.bfloat16)


def summed_turned(slabs, select_ref):
    return lax.dot_general(
        slabs, select_ref[...], (((0,), (0,)), ((), ())), preferred_element_type=jnp.float32
    )


def summed(slabs, turned_ref):
    return jnp.dot(turned_ref[...], slabs, preferred_element_type=jnp.float32)


def larger(most, part):
    return jnp.maximum(most, jnp.max(jnp.abs(part).reshape(-1, 8, NROW), axis=0))


def outer_tiles(slabs):
    return jnp.concatenate([slabs[:, :TILE], slabs[:, -TILE:]], axis=1)


def store_part(out_ref, other, slabs, select_ref, turned_ref, most):
    outer = summed_turned(outer_tiles(slabs), select_ref)
    out_ref[other, 0:TILE] = outer[:TILE]
    out_ref[other, OWN - TILE : OWN] = outer[TILE:]
    inner = summed(slabs[:, TILE : OWN - TILE], turned_ref)
    for tile in range(1, OWN // TILE - 1):
        part = inner[:, (tile - 1) * TILE : tile * TILE]
        out_ref[other, tile * TILE : (tile + 1) * TILE] = part
        most = larger(most, part)
    return outer[:HALO], outer[2 * TILE - HALO :], larger(most, outer)


def power_above(most):
    most = jnp.full((8, NROW), jnp.max(most), jnp.float32)
    return jnp.ceil(jnp.log2(jnp.maximum(most, 2.0**-100)))[0:1]


def far_kernel(slot_ref, slab_ref, out_ref, edges_ref, power_ref, held, select_ref, turned_ref, sems):
    relay = Relay()

    def fetches(other):
        band = relay.band_at(FAR, other)
        pieces = [
            (before(band) * OWN + OWN - TILE, TILE, 0),
            (band * OWN, OWN, TILE),
            (after(band) * OWN, TILE, TILE + OWN),
        ]
        return [
            pltpu.make_async_copy(
                slab_ref.at[:, :, pl.ds(pl.multiple_of(first, TILE), width)],
                held.at[other, :, :, pl.ds(to, width)],
                sems.at[other, piece],
            )
            for piece, (first, width, to) in enumerate(pieces)
        ]

    for other in range(SIDE):
        for copy in fetches(other):
            copy.start()
    fill_select(slot_ref, select_ref, turned_ref)

    def chunk(other, most):
        for copy in fetches(other):
            copy.wait()
        band = relay.band_at(FAR, other)
        slabs = held[other].reshape(SLOTS * BLK, OWN + 2 * TILE)
        low, high, most = store_part(
            out_ref, other, slabs[:, TILE : TILE + OWN], select_ref, turned_ref, most
        )
        edges_ref[other, 0:HALO] = high
        edges_ref[other, HALO:] = low
        outer = summed_turned(outer_tiles(slabs), select_ref)
        left, right = outer[TILE - HALO : TILE], outer[TILE : TILE + HALO]
        out_ref[other, OWN : OWN + HALO] = left
        out_ref[other, OWN + HALO :] = right
        return larger(larger(most, left), right)

    most = lax.fori_loop(0, SIDE, chunk, jnp.zeros((8, NROW), jnp.float32))
    power_ref[...] = power_above(most)


def near_kernel(slot_ref, slab_ref, far_edges_ref, *refs):
    out_refs, refs = refs[: len(NEAR)], refs[len(NEAR) :]
    power_ref, held, edges, select_ref, turned_ref, sems = refs
    relay = Relay()

    def band_of(slot):
        step = jnp.where(slot < SIDE, NEAR[0], jnp.where(slot < 2 * SIDE, NEAR[1], NEAR[2]))
        return relay.band_at(step, lax.rem(slot, SIDE))

    def fetch(slot):
        columns = pl.ds(pl.multiple_of(band_of(slot) * OWN, OWN), OWN)
        return pltpu.make_async_copy(slab_ref.at[:, :, columns], held.at[slot], sems.at[slot])

    for slot in range(len(NEAR) * SIDE):
        fetch(slot).start()
    fill_select(slot_ref, select_ref, turned_ref)
    for other in range(SIDE):
        band = relay.band_at(FAR, other)
        edges[relay.place(after(band)), 0:HALO] = far_edges_ref[other, 0:HALO]
        edges[relay.place(before(band)), HALO:] = far_edges_ref[other, HALO:]

    def chunks(index, most):
        def chunk(other, most):
            slot = SIDE * index + other
            fetch(slot).wait()
            slabs = held[slot].reshape(SLOTS * BLK, OWN)
            low, high, most = store_part(
                out_refs[index], other, slabs, select_ref, turned_ref, most
            )
            edges[relay.place(after(band_of(slot))), 0:HALO] = high
            edges[relay.place(before(band_of(slot))), HALO:] = low
            return most

        return lax.fori_loop(0, SIDE, chunk, most)

    most = jnp.zeros((8, NROW), jnp.float32)
    for index in range(len(NEAR)):
        most = chunks(index, most)
    for index, step in enumerate(NEAR):
        for other in range(SIDE):
            block = edges[SIDE * step + other]
            out_refs[index][other, OWN:] = block
            most = larger(most, block)
    power_ref[...] = power_above(most)


def sum_call(kernel, name, operands, parts, more, held, sems):
    vmem = pl.BlockSpec(memory_space=pltpu.VMEM)
    return pl.pallas_call(
        kernel,
        in_specs=[pl.BlockSpec(memory_space=pltpu.SMEM), pl.BlockSpec(memory_space=pl.ANY)]
        + [vmem] * (len(operands) - 2),
        out_specs=[vmem] * (parts + len(more)),
        out_shape=[pltpu.VMEM((SIDE, SPAN, NROW), jnp.float32)] * parts + more,
        scratch_shapes=held
        + [
            pltpu.VMEM((SLOTS * BLK, NROW), jnp.bfloat16),
            pltpu.VMEM((NROW, SLOTS * BLK), jnp.bfloat16),
            pltpu.SemaphoreType.DMA(sems),
        ],
        compiler_params=pltpu.CompilerParams(vmem_limit_bytes=VMEM_BYTES),
        name=name,
    )(*operands)


POWER = pltpu.VMEM((1, NROW), jnp.float32)
EDGES = pltpu.VMEM((BANDS, 2 * HALO, NROW), jnp.float32)


def far_sums(slabs, slot_block):
    held = pltpu.VMEM((SIDE, SLOTS, BLK, OWN + 2 * TILE), jnp.bfloat16)
    operands = (slot_block, slabs)
    edges = pltpu.VMEM((SIDE, 2 * HALO, NROW), jnp.float32)
    return sum_call(far_kernel, "far_sums", operands, 1, [edges, POWER], [held], (SIDE, 3))


def near_sums(slabs, slot_block, edges):
    count = SIDE * len(NEAR)
    held = pltpu.VMEM((count, SLOTS, BLK, OWN), jnp.bfloat16)
    operands = (slot_block, slabs, edges)
    return sum_call(near_kernel, "near_sums", operands, 3, [POWER], [held, EDGES], (count,))


STEPS = SPAN // 8


def relax_kernel(weight_ref, part_ref, out_ref, plain_ref, density_ref, even_ref, odd_ref, turned_ref):
    zero = jnp.zeros((8, NROW), jnp.float32)
    turned_ref[0:8] = zero
    turned_ref[8 + NROW :] = zero
    lane = lax.broadcasted_iota(jnp.int32, (8, NROW), 1)
    not_first = lane > 0
    not_last = lane < NROW - 1
    share = 1.0 / (4.0 + MASS)

    plain_ref[0:HALO] = part_ref[OWN : OWN + HALO]
    plain_ref[HALO + OWN :] = part_ref[OWN + HALO :]
    for tile in range(OWN // TILE):
        part = part_ref[tile * TILE : (tile + 1) * TILE]
        part = part if tile in (0, OWN // TILE - 1) else part.T
        plain_ref[HALO + tile * TILE : HALO + (tile + 1) * TILE] = part

    for t in range(STEPS):
        block = plain_ref[pl.ds(t, 8, stride=STEPS)]
        density_ref[8 * t : 8 * t + 8] = block
        even_ref[8 * t : 8 * t + 8] = block * share

    def sweep(src, dst):
        first = here = src[0:8]
        behind = pltpu.roll(src[8 * STEPS - 8 :], 1, 0)
        for t in range(STEPS):
            ahead = src[8 * t + 8 : 8 * t + 16] if t < STEPS - 1 else pltpu.roll(first, 7, 0)
            total = behind + ahead + density_ref[8 * t : 8 * t + 8]
            total += jnp.where(not_first, pltpu.roll(here, 1, 1), 0.0)
            total += jnp.where(not_last, pltpu.roll(here, NROW - 1, 1), 0.0)
            dst[8 * t : 8 * t + 8] = total * share
            behind, here = here, ahead

    def two_sweeps(_, carry):
        sweep(even_ref, odd_ref)
        sweep(odd_ref, even_ref)
        return carry

    lax.fori_loop(0, (SWEEPS - 1) // 2, two_sweeps, 0)
    sweep(even_ref, odd_ref)
    weight = weight_ref[0]
    for t in range(STEPS):
        plain_ref[pl.ds(t, 8, stride=STEPS)] = odd_ref[8 * t : 8 * t + 8] * weight
    for tile in range(OWN // TILE):
        first = HALO + tile * TILE
        turned_ref[8 : 8 + NROW] = plain_ref[first : first + TILE].T
        for band in range(BANDS):
            out_ref[BANDS - 1 - band, tile * ROWS : (tile + 1) * ROWS] = turned_ref[
                R * band + 7 : R * band + 7 + ROWS
            ]


def relaxed(density, weight):
    return pl.pallas_call(
        relax_kernel,
        in_specs=[
            pl.BlockSpec(memory_space=pltpu.SMEM),
            pl.BlockSpec(memory_space=pltpu.VMEM),
        ],
        out_specs=pl.BlockSpec(memory_space=pltpu.VMEM),
        out_shape=jax.ShapeDtypeStruct((BANDS, MSG, TILE), jnp.float32),
        scratch_shapes=[
            pltpu.VMEM((SPAN, NROW), jnp.float32),
            pltpu.VMEM((SPAN, NROW), jnp.float32),
            pltpu.VMEM((SPAN, NROW), jnp.float32),
            pltpu.VMEM((SPAN, NROW), jnp.float32),
            pltpu.VMEM((NROW + 16, TILE), jnp.float32),
        ],
        compiler_params=pltpu.CompilerParams(vmem_limit_bytes=24 * 2**20),
        name="relaxed",
    )(weight, density)


GROUP = OWN // TILE
PART = NCOL // SIDE


def plane_maps(ref, starts, is_first, is_last):
    mid, rise, both = [], [], []
    for start in starts:
        south, north = ref[pl.ds(start, R)], ref[pl.ds(start + 2, R)]
        mid.append(ref[pl.ds(start + 1, R)])
        rise.append(north - south)
        both.append(north + south)
    easts = [[pltpu.roll(x, TILE - 1, 1) for x in xs[1:]] for xs in (mid, rise)]
    wests = [[pltpu.roll(x, 1, 1) for x in xs[:-1]] for xs in (mid, rise)]
    maps = []
    for t in range(GROUP):
        east, rise_east = (jnp.where(is_last, e[t + 1], e[t]) for e in easts)
        west, rise_west = (jnp.where(is_first, w[t], w[t + 1]) for w in wests)
        twice = 2.0 * mid[t + 1]
        p11 = 1.0 - (east - twice + west)
        p22 = 1.0 - (both[t + 1] - twice)
        p12 = 0.25 * (rise_west - rise_east)
        maps.append((p11, p12, p22, 0.5 * (east - west), 0.5 * rise[t + 1]))
    return maps


def after_map(state, maps):
    a11, a12, a21, a22, s1, s2 = state
    p11, p12, p22, c1, c2 = maps
    return (
        a11 * p11 + a12 * p12,
        a11 * p12 + a12 * p22,
        a21 * p11 + a22 * p12,
        a21 * p12 + a22 * p22,
        a11 * c1 + a12 * c2 + s1,
        a21 * c1 + a22 * c2 + s2,
    )


def after_state(state, first):
    a11, a12, a21, a22, s1, s2 = state
    b11, b12, b21, b22, t1, t2 = first
    return (
        a11 * b11 + a12 * b21,
        a11 * b12 + a12 * b22,
        a21 * b11 + a22 * b21,
        a21 * b12 + a22 * b22,
        a11 * t1 + a12 * t2 + s1,
        a21 * t1 + a22 * t2 + s2,
    )


def chain_step(state_ref, out_ref, pieces, first_ref=None, final_ref=None, sems=None):
    lane = lax.broadcasted_iota(jnp.int32, (R, TILE), 1)
    is_first = lane == 0
    is_last = lane == TILE - 1

    def group_body(group, carry):
        here = pl.multiple_of(group * MSG, 8)
        behind = pl.multiple_of(lax.rem(group + 1, BANDS) * MSG, 8)
        ahead = pl.multiple_of(lax.rem(group + BANDS - 1, BANDS) * MSG, 8)
        starts = [behind + MSG - ROWS] + [here + t * ROWS for t in range(GROUP)] + [ahead]
        first = (BANDS - 1 - group) * OWN
        columns = [pl.ds(pl.multiple_of(first + t * TILE, TILE), TILE) for t in range(GROUP)]
        maps = [plane_maps(piece, starts, is_first, is_last) for piece in pieces]
        for t in range(GROUP):
            if state_ref is None:
                p11, p12, p22, c1, c2 = maps[0][t]
                state = (p11, p12, p12, p22, c1, c2)
                rest = maps[1:]
            else:
                state = tuple(state_ref[entry, :, columns[t]] for entry in range(6))
                rest = maps
            for one in rest:
                state = after_map(state, one[t])
            if first_ref is not None:
                state = after_state(state, [first_ref[entry, :, columns[t]] for entry in range(6)])
            if final_ref is not None:
                state = tuple(x - 1.0 if e in (0, 3) else x for e, x in enumerate(state))
            for entry in range(6):
                out_ref[entry, :, columns[t]] = state[entry]
        return carry

    def columns_of(part):
        return pl.ds(pl.multiple_of(part * PART, PART), PART)

    def copy_out(part):
        columns = columns_of(part)
        return pltpu.make_async_copy(
            out_ref.at[:, :, columns], final_ref.at[:, :, columns], sems.at[part]
        )

    def part_body(part, carry):
        for group in range(SIDE):
            group_body(part * SIDE + group, 0)
        if final_ref is not None:
            copy_out(SIDE - 1 - part).start()
        return carry

    lax.fori_loop(0, SIDE, part_body, 0)
    if final_ref is not None:
        for part in range(SIDE):
            copy_out(part).wait()


def recent_kernel(back, own_ref, other_ref, one_ref, one_other_ref, out_ref):
    me = lax.axis_index("plane")
    chip, core = me // 2, lax.rem(me, 2)
    for which in (0, 1):
        near = [own_ref, other_ref] if which else [own_ref]
        far = [one_ref, one_other_ref] if which else [one_other_ref, one_ref]

        @pl.when(jnp.logical_and(chip < back, core == which))
        def _():
            chain_step(None, out_ref, near)

        @pl.when(jnp.logical_and(chip >= back, core == which))
        def _():
            chain_step(None, out_ref, near + far)


def first_kernel(back, own_ref, other_ref, out_ref):
    me = lax.axis_index("plane")
    chip, core = me // 2, lax.rem(me, 2)
    for which in (0, 1):
        pieces = [own_ref, other_ref] if which else [other_ref, own_ref]

        @pl.when(jnp.logical_and(chip >= back, core == which))
        def _():
            chain_step(None, out_ref, pieces)


def finish_kernel(back, state_ref, own_ref, other_ref, first_ref, final_ref, out_ref, sems):
    me = lax.axis_index("plane")
    chip, core = me // 2, lax.rem(me, 2)
    final_ref = final_ref.at[0]

    @pl.when(chip < back)
    def _():
        chain_step(state_ref, out_ref, [], None, final_ref, sems)

    for which in (0, 1):
        pieces = [own_ref, other_ref] if which else [other_ref, own_ref]

        @pl.when(jnp.logical_and(chip == back, core == which))
        def _():
            chain_step(state_ref, out_ref, pieces, None, final_ref, sems)

        @pl.when(jnp.logical_and(chip > back, core == which))
        def _():
            chain_step(state_ref, out_ref, pieces, first_ref, final_ref, sems)


def chain_call(kernel, name, operands, shape, last=False):
    vmem = pl.BlockSpec(memory_space=pltpu.VMEM)
    scratch = [pltpu.VMEM((6, R, NCOL), jnp.float32), pltpu.SemaphoreType.DMA((SIDE,))]
    return pl.pallas_call(
        kernel,
        in_specs=[vmem] * len(operands),
        out_specs=pl.BlockSpec(memory_space=pl.ANY) if last else vmem,
        scratch_shapes=scratch if last else [],
        out_shape=jax.ShapeDtypeStruct(shape, jnp.float32),
        cost_estimate=pl.CostEstimate(
            flops=80 * R * NCOL,
            bytes_accessed=sum(4 * x.size for x in operands) + 24 * R * NCOL,
            transcendentals=0,
        ),
        compiler_params=pltpu.CompilerParams(vmem_limit_bytes=16 * 2**20),
        name=name,
    )(*operands)


def from_chip(block, back):
    return lax.ppermute(block, "plane", [(i, (i + 2 * back) % PLANES) for i in range(PLANES)])


def from_other_core(block):
    return lax.ppermute(block, "plane", [(i, i ^ 1) for i in range(PLANES)])


def exchanged(block, step, first):
    route = []
    for plane in range(PLANES):
        side = 1 if (plane % 2 == 0) == first else SIDE
        for band in range(BANDS):
            route.append((plane * BANDS + band, plane * BANDS + (band ^ (step * side))))
    return lax.ppermute(block, ("plane", "band"), route)


def coded(values, power):
    row = lax.broadcasted_iota(jnp.int32, values.shape, values.ndim - 2)
    scaled = values * jnp.exp2(TOP - power)
    return jnp.where(row == OWN, power, scaled).astype(jnp.float16)


def power_of(code):
    return code.reshape(-1, SPAN, NROW)[0, OWN : OWN + 1].astype(jnp.float32)


def decoded(code, factor):
    return code.astype(jnp.float32) * factor


def reduced_density(slabs, slot_block):
    far, edges, power = far_sums(slabs, slot_block)
    code = coded(far, power)
    code, edges = lax.optimization_barrier((code, edges))
    codes = {FAR: exchanged(code, FAR, True)}
    *parts, power = near_sums(slabs, slot_block, edges)
    parts = dict(zip(NEAR, parts))
    for step in NEAR[:2]:
        codes[step] = exchanged(coded(parts[step], power), step, True)
    powers = [power_of(codes[step]) for step in ORDER[:3]]
    power = functools.reduce(jnp.maximum, powers, power)
    factors = {step: jnp.exp2(x - TOP) for step, x in zip(ORDER, powers)}
    sums = {}
    for other in (2, 1, 3, 0):
        total = parts[0][other]
        for step in (3, 1, 2):
            total += decoded(codes[step][other], factors[step])
        sums[other] = total if other == 0 else exchanged(coded(total, power), other, False)
    for other in (2, 1, 3):
        total = sums[0]
        factor = jnp.exp2(power_of(sums[other]) - TOP)
        sums[0] = total + decoded(sums[other], factor)
    return sums[0]


def body(slabs, slot_block, lens_weight):
    density = reduced_density(slabs[0], slot_block)
    messages = relaxed(density, lens_weight)
    backwards = [list(range(BANDS))[::-1]]
    rows = lax.all_to_all(
        messages, "band", split_axis=0, concat_axis=0, axis_index_groups=backwards, tiled=True
    )
    rows = rows.reshape(BANDS * MSG, TILE)
    two, one, three = (from_chip(rows, back) for back in (2, 1, 3))
    shape = (6, R, NCOL)
    recent = functools.partial(recent_kernel, 1)
    operands = (rows, from_other_core(rows), one, from_other_core(one))
    recent = chain_call(recent, "chain_recent", operands, shape)
    first = functools.partial(first_kernel, 3)
    first = chain_call(first, "chain_first", (three, from_other_core(three)), shape)
    finish = functools.partial(finish_kernel, 2)
    operands = (recent, two, from_other_core(two), first)
    return chain_call(finish, "chain_finish", operands, (1,) + shape, last=True)


def solution(mesh):
    in_specs = (P("plane", "band", None, None), P("plane", "band"), P("plane"))
    out_specs = P("plane", None, "band", None)
    return jax.shard_map(body, mesh=mesh, in_specs=in_specs, out_specs=out_specs, check_vma=False)
```

```python
import functools

import jax
import jax.numpy as jnp
from jax import lax
from jax.experimental import pallas as pl
from jax.experimental.pallas import tpu as pltpu
from jax.sharding import PartitionSpec as P

NCOL = 8192
NROW = 128
R = 8
BLK = 4
SLOTS = 64
SWEEPS = 20
PLANES = 8
BANDS = 16
SIDE = 4
MASS = 0.05

OWN = NCOL // BANDS
HALO = 24
SPAN = OWN + 2 * HALO
TILE = 128
ROWS = R + 2
MSG = ROWS * OWN // TILE
TOP = 13.0
VMEM_BYTES = 53 * 2**20


FAR, NEAR = 2, (1, 3)
ORDER = (1, 3, 2, 0)


class Relay:
    def __init__(self):
        self.core = lax.rem(lax.axis_index("plane"), 2)
        self.me = lax.axis_index("band")

    def band_at(self, step, other):
        over_y = jnp.where(self.core == 0, other, step)
        over_z = jnp.where(self.core == 0, step, other)
        return self.me ^ (SIDE * over_y + over_z)

    def place(self, band):
        over_y, over_z = (self.me ^ band) // SIDE, (self.me ^ band) % SIDE
        return jnp.where(self.core == 0, SIDE * over_z + over_y, SIDE * over_y + over_z)


def before(band):
    return lax.rem(band + BANDS - 1, BANDS)


def after(band):
    return lax.rem(band + 1, BANDS)


def fill_select(slot_ref, slots, slot_sem, select_ref, turned_ref):
    pltpu.make_async_copy(slot_ref, slots, slot_sem).wait()
    lane = lax.broadcasted_iota(jnp.int32, (8, NROW), 1)
    sub = lax.broadcasted_iota(jnp.int32, (8, NROW), 0)
    picks = []
    for pair in range(SLOTS // 2):
        block = jnp.where(sub < BLK, slots[0, 2 * pair], slots[0, 2 * pair + 1])
        row = block * BLK + (sub & (BLK - 1))
        picks.append(jnp.where(lane == row, 1.0, 0.0))
    select = jnp.concatenate(picks, 0)
    select_ref[...] = select.astype(jnp.bfloat16)
    turned_ref[...] = select.T.astype(jnp.bfloat16)


def summed_turned(slabs, select_ref):
    return lax.dot_general(
        slabs, select_ref[...], (((0,), (0,)), ((), ())), preferred_element_type=jnp.float32
    )


def summed(slabs, turned_ref):
    return jnp.dot(turned_ref[...], slabs, preferred_element_type=jnp.float32)


def larger(most, part):
    return jnp.maximum(most, jnp.max(jnp.abs(part).reshape(-1, 8, NROW), axis=0))


def outer_tiles(slabs):
    return jnp.concatenate([slabs[:, :TILE], slabs[:, -TILE:]], axis=1)


def store_part(out_ref, other, slabs, select_ref, turned_ref, most):
    outer = summed_turned(outer_tiles(slabs), select_ref)
    out_ref[other, 0:TILE] = outer[:TILE]
    out_ref[other, OWN - TILE : OWN] = outer[TILE:]
    inner = summed(slabs[:, TILE : OWN - TILE], turned_ref)
    for tile in range(1, OWN // TILE - 1):
        part = inner[:, (tile - 1) * TILE : tile * TILE]
        out_ref[other, tile * TILE : (tile + 1) * TILE] = part
        most = larger(most, part)
    return outer[:HALO], outer[2 * TILE - HALO :], larger(most, outer)


def power_above(most):
    most = jnp.full((8, NROW), jnp.max(most), jnp.float32)
    return jnp.ceil(jnp.log2(jnp.maximum(most, 2.0**-100)))[0:1]


def window_kernel(step, slot_ref, slab_ref, out_ref, edges_ref, power_ref, *scratch):
    held, select_ref, turned_ref, slots, sems, slot_sem = scratch
    pltpu.make_async_copy(slot_ref, slots, slot_sem).start()
    relay = Relay()

    def fetch(other, act):
        band = relay.band_at(step, other)

        def copy(first, width, to, piece):
            return pltpu.make_async_copy(
                slab_ref.at[:, :, pl.ds(pl.multiple_of(first, TILE), width)],
                held.at[other, :, :, pl.ds(to, width)],
                sems.at[other, piece],
            )

        inside = jnp.logical_and(band > 0, band < BANDS - 1)

        @pl.when(inside)
        def _():
            act(copy(band * OWN - TILE, OWN + 2 * TILE, 0, 0))

        @pl.when(jnp.logical_not(inside))
        def _():
            act(copy(band * OWN, OWN, TILE, 0))
            act(copy(before(band) * OWN + OWN - TILE, TILE, 0, 1))
            act(copy(after(band) * OWN, TILE, TILE + OWN, 2))

    for other in range(SIDE):
        fetch(other, lambda copy: copy.start())
    fill_select(slot_ref, slots, slot_sem, select_ref, turned_ref)

    def chunk(other, most):
        fetch(other, lambda copy: copy.wait())
        slabs = held[other].reshape(SLOTS * BLK, OWN + 2 * TILE)
        low, high, most = store_part(
            out_ref, other, slabs[:, TILE : TILE + OWN], select_ref, turned_ref, most
        )
        edges_ref[other, 0:HALO] = high
        edges_ref[other, HALO:] = low
        outer = summed_turned(outer_tiles(slabs), select_ref)
        left, right = outer[TILE - HALO : TILE], outer[TILE : TILE + HALO]
        out_ref[other, OWN : OWN + HALO] = left
        out_ref[other, OWN + HALO :] = right
        return larger(larger(most, left), right)

    most = lax.fori_loop(0, SIDE, chunk, jnp.zeros((8, NROW), jnp.float32))
    power_ref[...] = power_above(most)


def own_kernel(slot_ref, slab_ref, weight_ref, out_ref, edges_ref, power_ref, row_ref, *scratch):
    row_ref[...] = jnp.full((1, NROW), weight_ref[0], jnp.float32)
    window_kernel(0, slot_ref, slab_ref, out_ref, edges_ref, power_ref, *scratch)


def near_kernel(slot_ref, slab_ref, far_edges_ref, *refs):
    out_refs, refs = refs[: len(NEAR)], refs[len(NEAR) :]
    power_ref, held, edges, far_edges, edge_sem, *refs = refs
    select_ref, turned_ref, slots, sems, slot_sem = refs
    pltpu.make_async_copy(slot_ref, slots, slot_sem).start()
    relay = Relay()

    def band_of(slot):
        step = jnp.where(slot < SIDE, NEAR[0], jnp.where(slot < 2 * SIDE, NEAR[1], 0))
        return relay.band_at(step, lax.rem(slot, SIDE))

    def fetch(slot):
        columns = pl.ds(pl.multiple_of(band_of(slot) * OWN, OWN), OWN)
        return pltpu.make_async_copy(slab_ref.at[:, :, columns], held.at[slot], sems.at[slot])

    for slot in range(len(NEAR) * SIDE + SIDE):
        fetch(slot).start()
    fill_select(slot_ref, slots, slot_sem, select_ref, turned_ref)
    far_copy = pltpu.make_async_copy(far_edges_ref, far_edges, edge_sem)
    far_copy.start()

    def chunks(index, most):
        def chunk(other, most):
            slot = SIDE * index + other
            fetch(slot).wait()
            slabs = held[slot].reshape(SLOTS * BLK, OWN)
            low, high, most = store_part(
                out_refs[index], other, slabs, select_ref, turned_ref, most
            )
            edges[relay.place(after(band_of(slot))), 0:HALO] = high
            edges[relay.place(before(band_of(slot))), HALO:] = low
            return most

        return lax.fori_loop(0, SIDE, chunk, most)

    most = jnp.zeros((8, NROW), jnp.float32)
    for index in range(len(NEAR)):
        most = chunks(index, most)

    def rim_chunk(other, carry):
        slot = len(NEAR) * SIDE + other
        fetch(slot).wait()
        band = band_of(slot)
        slabs = held[slot].reshape(SLOTS * BLK, OWN)
        outer = summed_turned(outer_tiles(slabs), select_ref)
        edges[relay.place(after(band)), 0:HALO] = outer[2 * TILE - HALO :]
        edges[relay.place(before(band)), HALO:] = outer[:HALO]
        return carry

    lax.fori_loop(0, SIDE, rim_chunk, 0)
    far_copy.wait()
    for other in range(SIDE):
        band = relay.band_at(FAR, other)
        edges[relay.place(after(band)), 0:HALO] = far_edges[other, 0:HALO]
        edges[relay.place(before(band)), HALO:] = far_edges[other, HALO:]
    for index, step in enumerate(NEAR):
        for other in range(SIDE):
            block = edges[SIDE * step + other]
            out_refs[index][other, OWN:] = block
            most = larger(most, block)
    power_ref[...] = power_above(most)


def sum_call(kernel, name, operands, parts, more, held, sems, third=pltpu.VMEM):
    vmem = pl.BlockSpec(memory_space=pltpu.VMEM)
    return pl.pallas_call(
        kernel,
        in_specs=[pl.BlockSpec(memory_space=pl.ANY)] * 2
        + [pl.BlockSpec(memory_space=third)] * (len(operands) - 2),
        out_specs=[vmem] * (parts + len(more)),
        out_shape=[pltpu.VMEM((SIDE, SPAN, NROW), jnp.float32)] * parts + more,
        scratch_shapes=held
        + [
            pltpu.VMEM((SLOTS * BLK, NROW), jnp.bfloat16),
            pltpu.VMEM((NROW, SLOTS * BLK), jnp.bfloat16),
            pltpu.SMEM((1, SLOTS), jnp.int32),
            pltpu.SemaphoreType.DMA(sems),
            pltpu.SemaphoreType.DMA,
        ],
        compiler_params=pltpu.CompilerParams(vmem_limit_bytes=VMEM_BYTES),
        name=name,
    )(*operands)


POWER = pltpu.VMEM((1, NROW), jnp.float32)
EDGES = pltpu.VMEM((BANDS, 2 * HALO, NROW), jnp.float32)


FAR_EDGES = pltpu.VMEM((SIDE, 2 * HALO, NROW), jnp.float32)
WINDOW = pltpu.VMEM((SIDE, SLOTS, BLK, OWN + 2 * TILE), jnp.bfloat16)


def far_sums(slabs, slot_block):
    kernel = functools.partial(window_kernel, FAR)
    more = [FAR_EDGES, POWER]
    return sum_call(kernel, "far_sums", (slot_block, slabs), 1, more, [WINDOW], (SIDE, 3))


def own_sums(slabs, slot_block, weight):
    operands = (slot_block, slabs, weight)
    more = [FAR_EDGES, POWER, POWER]
    return sum_call(own_kernel, "own_sums", operands, 1, more, [WINDOW], (SIDE, 3), pltpu.SMEM)


def near_sums(slabs, slot_block, edges):
    count = SIDE * len(NEAR) + SIDE
    held = pltpu.VMEM((count, SLOTS, BLK, OWN), jnp.bfloat16)
    operands = (slot_block, slabs, edges)
    scratch = [held, EDGES, FAR_EDGES, pltpu.SemaphoreType.DMA]
    return sum_call(near_kernel, "near_sums", operands, 2, [POWER], scratch, (count,), pl.ANY)


STEPS = SPAN // 8


def relax_kernel(weight_ref, part_ref, out_ref, plain_ref, density_ref, even_ref, odd_ref, turned_ref):
    zero = jnp.zeros((8, NROW), jnp.float32)
    turned_ref[0:8] = zero
    turned_ref[8 + NROW :] = zero
    lane = lax.broadcasted_iota(jnp.int32, (8, NROW), 1)
    not_first = lane > 0
    not_last = lane < NROW - 1
    share = 1.0 / (4.0 + MASS)

    plain_ref[0:HALO] = part_ref[OWN : OWN + HALO]
    plain_ref[HALO + OWN :] = part_ref[OWN + HALO :]
    for tile in range(OWN // TILE):
        part = part_ref[tile * TILE : (tile + 1) * TILE]
        part = part if tile in (0, OWN // TILE - 1) else part.T
        plain_ref[HALO + tile * TILE : HALO + (tile + 1) * TILE] = part

    for t in range(STEPS):
        block = plain_ref[pl.ds(t, 8, stride=STEPS)]
        density_ref[8 * t : 8 * t + 8] = block
        even_ref[8 * t : 8 * t + 8] = block * share

    def sweep(src, dst):
        first = here = src[0:8]
        behind = pltpu.roll(src[8 * STEPS - 8 :], 1, 0)
        for t in range(STEPS):
            ahead = src[8 * t + 8 : 8 * t + 16] if t < STEPS - 1 else pltpu.roll(first, 7, 0)
            total = behind + ahead + density_ref[8 * t : 8 * t + 8]
            total += jnp.where(not_first, pltpu.roll(here, 1, 1), 0.0)
            total += jnp.where(not_last, pltpu.roll(here, NROW - 1, 1), 0.0)
            dst[8 * t : 8 * t + 8] = total * share
            behind, here = here, ahead

    def two_sweeps(_, carry):
        sweep(even_ref, odd_ref)
        sweep(odd_ref, even_ref)
        return carry

    lax.fori_loop(0, (SWEEPS - 1) // 2, two_sweeps, 0)
    sweep(even_ref, odd_ref)
    weight = jnp.broadcast_to(weight_ref[...], (8, NROW))
    for t in range(STEPS):
        plain_ref[pl.ds(t, 8, stride=STEPS)] = odd_ref[8 * t : 8 * t + 8] * weight
    for tile in range(OWN // TILE):
        first = HALO + tile * TILE
        turned_ref[8 : 8 + NROW] = plain_ref[first : first + TILE].T
        for band in range(BANDS):
            out_ref[BANDS - 1 - band, tile * ROWS : (tile + 1) * ROWS] = turned_ref[
                R * band + 7 : R * band + 7 + ROWS
            ]


def relaxed(density, weight):
    return pl.pallas_call(
        relax_kernel,
        in_specs=[
            pl.BlockSpec(memory_space=pltpu.VMEM),
            pl.BlockSpec(memory_space=pltpu.VMEM),
        ],
        out_specs=pl.BlockSpec(memory_space=pltpu.VMEM),
        out_shape=jax.ShapeDtypeStruct((BANDS, MSG, TILE), jnp.float32),
        scratch_shapes=[
            pltpu.VMEM((SPAN, NROW), jnp.float32),
            pltpu.VMEM((SPAN, NROW), jnp.float32),
            pltpu.VMEM((SPAN, NROW), jnp.float32),
            pltpu.VMEM((SPAN, NROW), jnp.float32),
            pltpu.VMEM((NROW + 16, TILE), jnp.float32),
        ],
        compiler_params=pltpu.CompilerParams(vmem_limit_bytes=24 * 2**20),
        name="relaxed",
    )(weight, density)


GROUP = OWN // TILE
PART = NCOL // SIDE


def plane_maps(ref, starts, is_first, is_last):
    mid, rise, both = [], [], []
    for start in starts:
        south, north = ref[pl.ds(start, R)], ref[pl.ds(start + 2, R)]
        mid.append(ref[pl.ds(start + 1, R)])
        rise.append(north - south)
        both.append(north + south)
    easts = [[pltpu.roll(x, TILE - 1, 1) for x in xs[1:]] for xs in (mid, rise)]
    wests = [[pltpu.roll(x, 1, 1) for x in xs[:-1]] for xs in (mid, rise)]
    maps = []
    for t in range(GROUP):
        east, rise_east = (jnp.where(is_last, e[t + 1], e[t]) for e in easts)
        west, rise_west = (jnp.where(is_first, w[t], w[t + 1]) for w in wests)
        twice = 2.0 * mid[t + 1]
        p11 = 1.0 - (east - twice + west)
        p22 = 1.0 - (both[t + 1] - twice)
        p12 = 0.25 * (rise_west - rise_east)
        maps.append((p11, p12, p22, 0.5 * (east - west), 0.5 * rise[t + 1]))
    return maps


def after_map(state, maps):
    a11, a12, a21, a22, s1, s2 = state
    p11, p12, p22, c1, c2 = maps
    return (
        a11 * p11 + a12 * p12,
        a11 * p12 + a12 * p22,
        a21 * p11 + a22 * p12,
        a21 * p12 + a22 * p22,
        a11 * c1 + a12 * c2 + s1,
        a21 * c1 + a22 * c2 + s2,
    )


def after_state(state, first):
    a11, a12, a21, a22, s1, s2 = state
    b11, b12, b21, b22, t1, t2 = first
    return (
        a11 * b11 + a12 * b21,
        a11 * b12 + a12 * b22,
        a21 * b11 + a22 * b21,
        a21 * b12 + a22 * b22,
        a11 * t1 + a12 * t2 + s1,
        a21 * t1 + a22 * t2 + s2,
    )


def chain_step(state_ref, out_ref, pieces, first_ref=None, final_ref=None, sems=None):
    lane = lax.broadcasted_iota(jnp.int32, (R, TILE), 1)
    is_first = lane == 0
    is_last = lane == TILE - 1

    def group_body(group, carry):
        here = pl.multiple_of(group * MSG, 8)
        behind = pl.multiple_of(lax.rem(group + 1, BANDS) * MSG, 8)
        ahead = pl.multiple_of(lax.rem(group + BANDS - 1, BANDS) * MSG, 8)
        starts = [behind + MSG - ROWS] + [here + t * ROWS for t in range(GROUP)] + [ahead]
        first = (BANDS - 1 - group) * OWN
        columns = [pl.ds(pl.multiple_of(first + t * TILE, TILE), TILE) for t in range(GROUP)]
        maps = [plane_maps(piece, starts, is_first, is_last) for piece in pieces]
        for t in range(GROUP):
            if state_ref is None:
                p11, p12, p22, c1, c2 = maps[0][t]
                state = (p11, p12, p12, p22, c1, c2)
                rest = maps[1:]
            else:
                state = tuple(state_ref[entry, :, columns[t]] for entry in range(6))
                rest = maps
            for one in rest:
                state = after_map(state, one[t])
            if first_ref is not None:
                state = after_state(state, [first_ref[entry, :, columns[t]] for entry in range(6)])
            if final_ref is not None:
                state = tuple(x - 1.0 if e in (0, 3) else x for e, x in enumerate(state))
            for entry in range(6):
                out_ref[entry, :, columns[t]] = state[entry]
        return carry

    def columns_of(part):
        return pl.ds(pl.multiple_of(part * PART, PART), PART)

    def copy_out(part):
        columns = columns_of(part)
        return pltpu.make_async_copy(
            out_ref.at[:, :, columns], final_ref.at[:, :, columns], sems.at[part]
        )

    def part_body(part, carry):
        for group in range(SIDE):
            group_body(part * SIDE + group, 0)
        if final_ref is not None:
            copy_out(SIDE - 1 - part).start()
        return carry

    lax.fori_loop(0, SIDE, part_body, 0)
    if final_ref is not None:
        for part in range(SIDE):
            copy_out(part).wait()


def recent_kernel(back, own_ref, other_ref, one_ref, one_other_ref, out_ref):
    me = lax.axis_index("plane")
    chip, core = me // 2, lax.rem(me, 2)
    for which in (0, 1):
        near = [own_ref, other_ref] if which else [own_ref]
        far = [one_ref, one_other_ref] if which else [one_other_ref, one_ref]

        @pl.when(jnp.logical_and(chip < back, core == which))
        def _():
            chain_step(None, out_ref, near)

        @pl.when(jnp.logical_and(chip >= back, core == which))
        def _():
            chain_step(None, out_ref, near + far)


def first_kernel(back, own_ref, other_ref, out_ref):
    me = lax.axis_index("plane")
    chip, core = me // 2, lax.rem(me, 2)
    for which in (0, 1):
        pieces = [own_ref, other_ref] if which else [other_ref, own_ref]

        @pl.when(jnp.logical_and(chip >= back, core == which))
        def _():
            chain_step(None, out_ref, pieces)


def finish_kernel(back, state_ref, own_ref, other_ref, first_ref, final_ref, out_ref, sems):
    me = lax.axis_index("plane")
    chip, core = me // 2, lax.rem(me, 2)
    final_ref = final_ref.at[0]

    @pl.when(chip < back)
    def _():
        chain_step(state_ref, out_ref, [], None, final_ref, sems)

    for which in (0, 1):
        pieces = [own_ref, other_ref] if which else [other_ref, own_ref]

        @pl.when(jnp.logical_and(chip == back, core == which))
        def _():
            chain_step(state_ref, out_ref, pieces, None, final_ref, sems)

        @pl.when(jnp.logical_and(chip > back, core == which))
        def _():
            chain_step(state_ref, out_ref, pieces, first_ref, final_ref, sems)


def chain_call(kernel, name, operands, shape, last=False):
    vmem = pl.BlockSpec(memory_space=pltpu.VMEM)
    scratch = [pltpu.VMEM((6, R, NCOL), jnp.float32), pltpu.SemaphoreType.DMA((SIDE,))]
    return pl.pallas_call(
        kernel,
        in_specs=[vmem] * len(operands),
        out_specs=pl.BlockSpec(memory_space=pl.ANY) if last else vmem,
        scratch_shapes=scratch if last else [],
        out_shape=jax.ShapeDtypeStruct(shape, jnp.float32),
        cost_estimate=pl.CostEstimate(
            flops=80 * R * NCOL,
            bytes_accessed=sum(4 * x.size for x in operands) + 24 * R * NCOL,
            transcendentals=0,
        ),
        compiler_params=pltpu.CompilerParams(vmem_limit_bytes=16 * 2**20),
        name=name,
    )(*operands)


def from_chip(block, back):
    return lax.ppermute(block, "plane", [(i, (i + 2 * back) % PLANES) for i in range(PLANES)])


def from_other_core(block):
    return lax.ppermute(block, "plane", [(i, i ^ 1) for i in range(PLANES)])


def exchanged(block, step, first):
    route = []
    for plane in range(PLANES):
        side = 1 if (plane % 2 == 0) == first else SIDE
        for band in range(BANDS):
            route.append((plane * BANDS + band, plane * BANDS + (band ^ (step * side))))
    return lax.ppermute(block, ("plane", "band"), route)


def coded(values, power):
    row = lax.broadcasted_iota(jnp.int32, values.shape, values.ndim - 2)
    scaled = values * jnp.exp2(TOP - power)
    return jnp.where(row == OWN, power, scaled).astype(jnp.float16)


def power_of(code):
    return code.reshape(-1, SPAN, NROW)[0, OWN : OWN + 1].astype(jnp.float32)


def decoded(code, factor):
    return code.astype(jnp.float32) * factor


def reduced_density(slabs, slot_block, weight):
    far, edges, power = far_sums(slabs, slot_block)
    code = coded(far, power)
    code, later_slots = lax.optimization_barrier((code, slot_block))
    codes = {FAR: exchanged(code, FAR, True)}
    *parts, power = near_sums(slabs, later_slots, edges)
    parts = dict(zip(NEAR, parts))
    for step in NEAR:
        codes[step] = exchanged(coded(parts[step], power), step, True)
    parts[0], _, power, weight = own_sums(slabs, slot_block, weight)
    powers = [power_of(codes[step]) for step in ORDER[:3]]
    power = functools.reduce(jnp.maximum, powers, power)
    factors = {step: jnp.exp2(x - TOP) for step, x in zip(ORDER, powers)}
    sums = {}
    for other in (2, 1, 3, 0):
        total = parts[0][other]
        for step in (3, 1, 2):
            total += decoded(codes[step][other], factors[step])
        sums[other] = total if other == 0 else exchanged(coded(total, power), other, False)
    for other in (2, 1, 3):
        total = sums[0]
        factor = jnp.exp2(power_of(sums[other]) - TOP)
        sums[0] = total + decoded(sums[other], factor)
    return sums[0], weight


def body(slabs, slot_block, lens_weight):
    density, weight = reduced_density(slabs[0], slot_block, lens_weight)
    messages = relaxed(density, weight)
    backwards = [list(range(BANDS))[::-1]]
    rows = lax.all_to_all(
        messages, "band", split_axis=0, concat_axis=0, axis_index_groups=backwards, tiled=True
    )
    rows = rows.reshape(BANDS * MSG, TILE)
    two, one, three = (from_chip(rows, back) for back in (2, 1, 3))
    shape = (6, R, NCOL)
    recent = functools.partial(recent_kernel, 1)
    operands = (rows, from_other_core(rows), one, from_other_core(one))
    recent = chain_call(recent, "chain_recent", operands, shape)
    first = functools.partial(first_kernel, 3)
    first = chain_call(first, "chain_first", (three, from_other_core(three)), shape)
    finish = functools.partial(finish_kernel, 2)
    operands = (recent, two, from_other_core(two), first)
    return chain_call(finish, "chain_finish", operands, (1,) + shape, last=True)


def solution(mesh):
    in_specs = (P("plane", "band", None, None), P("plane", "band"), P("plane"))
    out_specs = P("plane", None, "band", None)
    return jax.shard_map(body, mesh=mesh, in_specs=in_specs, out_specs=out_specs, check_vma=False)
```

```python
import functools

import jax
import jax.numpy as jnp
from jax import lax
from jax.experimental import pallas as pl
from jax.experimental.pallas import tpu as pltpu
from jax.sharding import PartitionSpec as P

NCOL = 8192
NROW = 128
R = 8
BLK = 4
SLOTS = 64
SWEEPS = 20
PLANES = 8
BANDS = 16
SIDE = 4
MASS = 0.05

OWN = NCOL // BANDS
HALO = 24
SPAN = OWN + 2 * HALO
TILE = 128
ROWS = R + 2
MSG = ROWS * OWN // TILE
TOP = 13.0
VMEM_BYTES = 53 * 2**20


FAR, NEAR = 2, (1, 3)
ORDER = (1, 3, 2, 0)


class Relay:
    def __init__(self):
        self.core = lax.rem(lax.axis_index("plane"), 2)
        self.me = lax.axis_index("band")

    def band_at(self, step, other):
        over_y = jnp.where(self.core == 0, other, step)
        over_z = jnp.where(self.core == 0, step, other)
        return self.me ^ (SIDE * over_y + over_z)

    def place(self, band):
        over_y, over_z = (self.me ^ band) // SIDE, (self.me ^ band) % SIDE
        return jnp.where(self.core == 0, SIDE * over_z + over_y, SIDE * over_y + over_z)


def before(band):
    return lax.rem(band + BANDS - 1, BANDS)


def after(band):
    return lax.rem(band + 1, BANDS)


def fill_select(slot_ref, slots, slot_sem, select_ref, turned_ref):
    pltpu.make_async_copy(slot_ref, slots, slot_sem).wait()
    lane = lax.broadcasted_iota(jnp.int32, (8, NROW), 1)
    sub = lax.broadcasted_iota(jnp.int32, (8, NROW), 0)
    picks = []
    for pair in range(SLOTS // 2):
        block = jnp.where(sub < BLK, slots[0, 2 * pair], slots[0, 2 * pair + 1])
        row = block * BLK + (sub & (BLK - 1))
        picks.append(jnp.where(lane == row, 1.0, 0.0))
    select = jnp.concatenate(picks, 0)
    select_ref[...] = select.astype(jnp.bfloat16)
    turned_ref[...] = select.T.astype(jnp.bfloat16)


def summed_turned(slabs, select_ref):
    return lax.dot_general(
        slabs, select_ref[...], (((0,), (0,)), ((), ())), preferred_element_type=jnp.float32
    )


def summed(slabs, turned_ref):
    return jnp.dot(turned_ref[...], slabs, preferred_element_type=jnp.float32)


def larger(most, part):
    return jnp.maximum(most, jnp.max(jnp.abs(part).reshape(-1, 8, NROW), axis=0))


def outer_tiles(slabs):
    return jnp.concatenate([slabs[:, :TILE], slabs[:, -TILE:]], axis=1)


def store_part(out_ref, other, slabs, select_ref, turned_ref, most):
    outer = summed_turned(outer_tiles(slabs), select_ref)
    out_ref[other, 0:TILE] = outer[:TILE]
    out_ref[other, OWN - TILE : OWN] = outer[TILE:]
    inner = summed(slabs[:, TILE : OWN - TILE], turned_ref)
    for tile in range(1, OWN // TILE - 1):
        part = inner[:, (tile - 1) * TILE : tile * TILE]
        out_ref[other, tile * TILE : (tile + 1) * TILE] = part
        most = larger(most, part)
    return outer[:HALO], outer[2 * TILE - HALO :], larger(most, outer)


def power_above(most):
    most = jnp.full((8, NROW), jnp.max(most), jnp.float32)
    return jnp.ceil(jnp.log2(jnp.maximum(most, 2.0**-100)))[0:1]


def window_kernel(step, slot_ref, slab_ref, out_ref, edges_ref, power_ref, *scratch):
    held, select_ref, turned_ref, slots, sems, slot_sem = scratch
    pltpu.make_async_copy(slot_ref, slots, slot_sem).start()
    relay = Relay()

    def fetch(other, act):
        band = relay.band_at(step, other)

        def copy(first, width, to, piece):
            return pltpu.make_async_copy(
                slab_ref.at[:, :, pl.ds(pl.multiple_of(first, TILE), width)],
                held.at[other, :, :, pl.ds(to, width)],
                sems.at[other, piece],
            )

        inside = jnp.logical_and(band > 0, band < BANDS - 1)

        @pl.when(inside)
        def _():
            act(copy(band * OWN - TILE, OWN + 2 * TILE, 0, 0))

        @pl.when(jnp.logical_not(inside))
        def _():
            act(copy(band * OWN, OWN, TILE, 0))
            act(copy(before(band) * OWN + OWN - TILE, TILE, 0, 1))
            act(copy(after(band) * OWN, TILE, TILE + OWN, 2))

    for other in range(SIDE):
        fetch(other, lambda copy: copy.start())
    fill_select(slot_ref, slots, slot_sem, select_ref, turned_ref)

    def chunk(other, most):
        fetch(other, lambda copy: copy.wait())
        slabs = held[other].reshape(SLOTS * BLK, OWN + 2 * TILE)
        low, high, most = store_part(
            out_ref, other, slabs[:, TILE : TILE + OWN], select_ref, turned_ref, most
        )
        edges_ref[other, 0:HALO] = high
        edges_ref[other, HALO:] = low
        outer = summed_turned(outer_tiles(slabs), select_ref)
        left, right = outer[TILE - HALO : TILE], outer[TILE : TILE + HALO]
        out_ref[other, OWN : OWN + HALO] = left
        out_ref[other, OWN + HALO :] = right
        return larger(larger(most, left), right)

    most = lax.fori_loop(0, SIDE, chunk, jnp.zeros((8, NROW), jnp.float32))
    power_ref[...] = power_above(most)


def own_kernel(slot_ref, slab_ref, weight_ref, out_ref, edges_ref, power_ref, row_ref, *scratch):
    row_ref[...] = jnp.full((1, NROW), weight_ref[0], jnp.float32)
    window_kernel(0, slot_ref, slab_ref, out_ref, edges_ref, power_ref, *scratch)


def near_kernel(slot_ref, slab_ref, far_edges_ref, *refs):
    out_refs, refs = refs[: len(NEAR)], refs[len(NEAR) :]
    power_ref, held, edges, far_edges, edge_sem, *refs = refs
    select_ref, turned_ref, slots, sems, slot_sem = refs
    pltpu.make_async_copy(slot_ref, slots, slot_sem).start()
    relay = Relay()

    def band_of(slot):
        step = jnp.where(slot < SIDE, NEAR[0], jnp.where(slot < 2 * SIDE, NEAR[1], 0))
        return relay.band_at(step, lax.rem(slot, SIDE))

    def fetch(slot):
        columns = pl.ds(pl.multiple_of(band_of(slot) * OWN, OWN), OWN)
        return pltpu.make_async_copy(slab_ref.at[:, :, columns], held.at[slot], sems.at[slot])

    for slot in range(len(NEAR) * SIDE + SIDE):
        fetch(slot).start()
    fill_select(slot_ref, slots, slot_sem, select_ref, turned_ref)
    far_copy = pltpu.make_async_copy(far_edges_ref, far_edges, edge_sem)
    far_copy.start()

    def chunks(index, most):
        def chunk(other, most):
            slot = SIDE * index + other
            fetch(slot).wait()
            slabs = held[slot].reshape(SLOTS * BLK, OWN)
            low, high, most = store_part(
                out_refs[index], other, slabs, select_ref, turned_ref, most
            )
            edges[relay.place(after(band_of(slot))), 0:HALO] = high
            edges[relay.place(before(band_of(slot))), HALO:] = low
            return most

        return lax.fori_loop(0, SIDE, chunk, most)

    most = jnp.zeros((8, NROW), jnp.float32)
    for index in range(len(NEAR)):
        most = chunks(index, most)

    def rim_chunk(other, carry):
        slot = len(NEAR) * SIDE + other
        fetch(slot).wait()
        band = band_of(slot)
        slabs = held[slot].reshape(SLOTS * BLK, OWN)
        outer = summed_turned(outer_tiles(slabs), select_ref)
        edges[relay.place(after(band)), 0:HALO] = outer[2 * TILE - HALO :]
        edges[relay.place(before(band)), HALO:] = outer[:HALO]
        return carry

    lax.fori_loop(0, SIDE, rim_chunk, 0)
    far_copy.wait()
    for other in range(SIDE):
        band = relay.band_at(FAR, other)
        edges[relay.place(after(band)), 0:HALO] = far_edges[other, 0:HALO]
        edges[relay.place(before(band)), HALO:] = far_edges[other, HALO:]
    for index, step in enumerate(NEAR):
        for other in range(SIDE):
            block = edges[SIDE * step + other]
            out_refs[index][other, OWN:] = block
            most = larger(most, block)
    power_ref[...] = power_above(most)


def sum_call(kernel, name, operands, parts, more, held, sems, third=pltpu.VMEM):
    vmem = pl.BlockSpec(memory_space=pltpu.VMEM)
    return pl.pallas_call(
        kernel,
        in_specs=[pl.BlockSpec(memory_space=pl.ANY)] * 2
        + [pl.BlockSpec(memory_space=third)] * (len(operands) - 2),
        out_specs=[vmem] * (parts + len(more)),
        out_shape=[pltpu.VMEM((SIDE, SPAN, NROW), jnp.float32)] * parts + more,
        scratch_shapes=held
        + [
            pltpu.VMEM((SLOTS * BLK, NROW), jnp.bfloat16),
            pltpu.VMEM((NROW, SLOTS * BLK), jnp.bfloat16),
            pltpu.SMEM((1, SLOTS), jnp.int32),
            pltpu.SemaphoreType.DMA(sems),
            pltpu.SemaphoreType.DMA,
        ],
        compiler_params=pltpu.CompilerParams(vmem_limit_bytes=VMEM_BYTES),
        name=name,
    )(*operands)


POWER = pltpu.VMEM((1, NROW), jnp.float32)
EDGES = pltpu.VMEM((BANDS, 2 * HALO, NROW), jnp.float32)


FAR_EDGES = pltpu.VMEM((SIDE, 2 * HALO, NROW), jnp.float32)
WINDOW = pltpu.VMEM((SIDE, SLOTS, BLK, OWN + 2 * TILE), jnp.bfloat16)


def far_sums(slabs, slot_block):
    kernel = functools.partial(window_kernel, FAR)
    more = [FAR_EDGES, POWER]
    return sum_call(kernel, "far_sums", (slot_block, slabs), 1, more, [WINDOW], (SIDE, 3))


def own_sums(slabs, slot_block, weight):
    operands = (slot_block, slabs, weight)
    more = [FAR_EDGES, POWER, POWER]
    return sum_call(own_kernel, "own_sums", operands, 1, more, [WINDOW], (SIDE, 3), pltpu.SMEM)


def near_sums(slabs, slot_block, edges):
    count = SIDE * len(NEAR) + SIDE
    held = pltpu.VMEM((count, SLOTS, BLK, OWN), jnp.bfloat16)
    operands = (slot_block, slabs, edges)
    scratch = [held, EDGES, FAR_EDGES, pltpu.SemaphoreType.DMA]
    return sum_call(near_kernel, "near_sums", operands, 2, [POWER], scratch, (count,), pl.ANY)


STEPS = SPAN // 8


def relax_kernel(weight_ref, part_ref, out_ref, plain_ref, density_ref, even_ref, odd_ref, turned_ref):
    zero = jnp.zeros((8, NROW), jnp.float32)
    turned_ref[0:8] = zero
    turned_ref[8 + NROW :] = zero
    lane = lax.broadcasted_iota(jnp.int32, (8, NROW), 1)
    not_first = lane > 0
    not_last = lane < NROW - 1
    share = 1.0 / (4.0 + MASS)

    plain_ref[0:HALO] = part_ref[OWN : OWN + HALO]
    plain_ref[HALO + OWN :] = part_ref[OWN + HALO :]
    for tile in range(OWN // TILE):
        part = part_ref[tile * TILE : (tile + 1) * TILE]
        part = part if tile in (0, OWN // TILE - 1) else part.T
        plain_ref[HALO + tile * TILE : HALO + (tile + 1) * TILE] = part

    for t in range(STEPS):
        block = plain_ref[pl.ds(t, 8, stride=STEPS)]
        density_ref[8 * t : 8 * t + 8] = block
        even_ref[8 * t : 8 * t + 8] = block * share

    def sweep(src, dst):
        first = here = src[0:8]
        behind = pltpu.roll(src[8 * STEPS - 8 :], 1, 0)
        for t in range(STEPS):
            ahead = src[8 * t + 8 : 8 * t + 16] if t < STEPS - 1 else pltpu.roll(first, 7, 0)
            total = behind + ahead + density_ref[8 * t : 8 * t + 8]
            total += jnp.where(not_first, pltpu.roll(here, 1, 1), 0.0)
            total += jnp.where(not_last, pltpu.roll(here, NROW - 1, 1), 0.0)
            dst[8 * t : 8 * t + 8] = total * share
            behind, here = here, ahead

    def two_sweeps(_, carry):
        sweep(even_ref, odd_ref)
        sweep(odd_ref, even_ref)
        return carry

    lax.fori_loop(0, (SWEEPS - 1) // 2, two_sweeps, 0)
    sweep(even_ref, odd_ref)
    weight = jnp.broadcast_to(weight_ref[...], (8, NROW))
    for t in range(STEPS):
        plain_ref[pl.ds(t, 8, stride=STEPS)] = odd_ref[8 * t : 8 * t + 8] * weight
    for tile in range(OWN // TILE):
        first = HALO + tile * TILE
        turned_ref[8 : 8 + NROW] = plain_ref[first : first + TILE].T
        for band in range(BANDS):
            out_ref[BANDS - 1 - band, tile * ROWS : (tile + 1) * ROWS] = turned_ref[
                R * band + 7 : R * band + 7 + ROWS
            ]


def relaxed(density, weight):
    return pl.pallas_call(
        relax_kernel,
        in_specs=[
            pl.BlockSpec(memory_space=pltpu.VMEM),
            pl.BlockSpec(memory_space=pltpu.VMEM),
        ],
        out_specs=pl.BlockSpec(memory_space=pltpu.VMEM),
        out_shape=jax.ShapeDtypeStruct((BANDS, MSG, TILE), jnp.float32),
        scratch_shapes=[
            pltpu.VMEM((SPAN, NROW), jnp.float32),
            pltpu.VMEM((SPAN, NROW), jnp.float32),
            pltpu.VMEM((SPAN, NROW), jnp.float32),
            pltpu.VMEM((SPAN, NROW), jnp.float32),
            pltpu.VMEM((NROW + 16, TILE), jnp.float32),
        ],
        compiler_params=pltpu.CompilerParams(vmem_limit_bytes=24 * 2**20),
        name="relaxed",
    )(weight, density)


GROUP = OWN // TILE
PART = NCOL // SIDE


def plane_maps(ref, starts, is_first, is_last):
    mid, rise, both = [], [], []
    for start in starts:
        south, north = ref[pl.ds(start, R)], ref[pl.ds(start + 2, R)]
        mid.append(ref[pl.ds(start + 1, R)])
        rise.append(north - south)
        both.append(north + south)
    easts = [[pltpu.roll(x, TILE - 1, 1) for x in xs[1:]] for xs in (mid, rise)]
    wests = [[pltpu.roll(x, 1, 1) for x in xs[:-1]] for xs in (mid, rise)]
    maps = []
    for t in range(GROUP):
        east, rise_east = (jnp.where(is_last, e[t + 1], e[t]) for e in easts)
        west, rise_west = (jnp.where(is_first, w[t], w[t + 1]) for w in wests)
        twice = 2.0 * mid[t + 1]
        p11 = 1.0 - (east - twice + west)
        p22 = 1.0 - (both[t + 1] - twice)
        p12 = 0.25 * (rise_west - rise_east)
        maps.append((p11, p12, p22, 0.5 * (east - west), 0.5 * rise[t + 1]))
    return maps


def after_map(state, maps):
    a11, a12, a21, a22, s1, s2 = state
    p11, p12, p22, c1, c2 = maps
    return (
        a11 * p11 + a12 * p12,
        a11 * p12 + a12 * p22,
        a21 * p11 + a22 * p12,
        a21 * p12 + a22 * p22,
        a11 * c1 + a12 * c2 + s1,
        a21 * c1 + a22 * c2 + s2,
    )


def after_state(state, first):
    a11, a12, a21, a22, s1, s2 = state
    b11, b12, b21, b22, t1, t2 = first
    return (
        a11 * b11 + a12 * b21,
        a11 * b12 + a12 * b22,
        a21 * b11 + a22 * b21,
        a21 * b12 + a22 * b22,
        a11 * t1 + a12 * t2 + s1,
        a21 * t1 + a22 * t2 + s2,
    )


def chain_step(state_ref, out_ref, pieces, middle_ref=None, final_ref=None, sems=None):
    lane = lax.broadcasted_iota(jnp.int32, (R, TILE), 1)
    is_first = lane == 0
    is_last = lane == TILE - 1

    def group_body(group, carry):
        here = pl.multiple_of(group * MSG, 8)
        behind = pl.multiple_of(lax.rem(group + 1, BANDS) * MSG, 8)
        ahead = pl.multiple_of(lax.rem(group + BANDS - 1, BANDS) * MSG, 8)
        starts = [behind + MSG - ROWS] + [here + t * ROWS for t in range(GROUP)] + [ahead]
        first = (BANDS - 1 - group) * OWN
        columns = [pl.ds(pl.multiple_of(first + t * TILE, TILE), TILE) for t in range(GROUP)]
        maps = [plane_maps(piece, starts, is_first, is_last) for piece in pieces]
        for t in range(GROUP):
            if state_ref is None:
                p11, p12, p22, c1, c2 = maps[0][t]
                state = (p11, p12, p12, p22, c1, c2)
                rest = maps[1:]
            else:
                state = tuple(state_ref[entry, :, columns[t]] for entry in range(6))
                rest = maps
            if middle_ref is not None:
                middle = [middle_ref[entry, :, columns[t]] for entry in range(6)]
                state = after_state(state, middle)
            for one in rest:
                state = after_map(state, one[t])
            if final_ref is not None:
                state = tuple(x - 1.0 if e in (0, 3) else x for e, x in enumerate(state))
            for entry in range(6):
                out_ref[entry, :, columns[t]] = state[entry]
        return carry

    def columns_of(part):
        return pl.ds(pl.multiple_of(part * PART, PART), PART)

    def copy_out(part):
        columns = columns_of(part)
        return pltpu.make_async_copy(
            out_ref.at[:, :, columns], final_ref.at[:, :, columns], sems.at[part]
        )

    def part_body(part, carry):
        for group in range(SIDE):
            group_body(part * SIDE + group, 0)
        if final_ref is not None:
            copy_out(SIDE - 1 - part).start()
        return carry

    lax.fori_loop(0, SIDE, part_body, 0)
    if final_ref is not None:
        for part in range(SIDE):
            copy_out(part).wait()


def recent_kernel(back, own_ref, other_ref, one_ref, one_other_ref, out_ref):
    me = lax.axis_index("plane")
    chip, core = me // 2, lax.rem(me, 2)
    for which in (0, 1):
        near = [own_ref, other_ref] if which else [own_ref]
        far = [one_ref, one_other_ref] if which else [one_other_ref, one_ref]

        @pl.when(jnp.logical_and(chip < back, core == which))
        def _():
            chain_step(None, out_ref, near)

        @pl.when(jnp.logical_and(chip >= back, core == which))
        def _():
            chain_step(None, out_ref, near + far)


def middle_kernel(back, own_ref, other_ref, out_ref):
    me = lax.axis_index("plane")
    chip, core = me // 2, lax.rem(me, 2)
    for which in (0, 1):
        pieces = [own_ref, other_ref] if which else [other_ref, own_ref]

        @pl.when(jnp.logical_and(chip >= back, core == which))
        def _():
            chain_step(None, out_ref, pieces)


def finish_kernel(back, state_ref, own_ref, other_ref, middle_ref, final_ref, out_ref, sems):
    me = lax.axis_index("plane")
    chip, core = me // 2, lax.rem(me, 2)
    final_ref = final_ref.at[0]

    @pl.when(chip < back - 1)
    def _():
        chain_step(state_ref, out_ref, [], None, final_ref, sems)

    @pl.when(chip == back - 1)
    def _():
        chain_step(state_ref, out_ref, [], middle_ref, final_ref, sems)

    for which in (0, 1):
        pieces = [own_ref, other_ref] if which else [other_ref, own_ref]

        @pl.when(jnp.logical_and(chip >= back, core == which))
        def _():
            chain_step(state_ref, out_ref, pieces, middle_ref, final_ref, sems)


def chain_call(kernel, name, operands, shape, last=False):
    vmem = pl.BlockSpec(memory_space=pltpu.VMEM)
    scratch = [pltpu.VMEM((6, R, NCOL), jnp.float32), pltpu.SemaphoreType.DMA((SIDE,))]
    return pl.pallas_call(
        kernel,
        in_specs=[vmem] * len(operands),
        out_specs=pl.BlockSpec(memory_space=pl.ANY) if last else vmem,
        scratch_shapes=scratch if last else [],
        out_shape=jax.ShapeDtypeStruct(shape, jnp.float32),
        cost_estimate=pl.CostEstimate(
            flops=80 * R * NCOL,
            bytes_accessed=sum(4 * x.size for x in operands) + 24 * R * NCOL,
            transcendentals=0,
        ),
        compiler_params=pltpu.CompilerParams(vmem_limit_bytes=16 * 2**20),
        name=name,
    )(*operands)


def from_chip(block, back):
    return lax.ppermute(block, "plane", [(i, (i + 2 * back) % PLANES) for i in range(PLANES)])


def from_other_core(block):
    return lax.ppermute(block, "plane", [(i, i ^ 1) for i in range(PLANES)])


def exchanged(block, step, first):
    route = []
    for plane in range(PLANES):
        side = 1 if (plane % 2 == 0) == first else SIDE
        for band in range(BANDS):
            route.append((plane * BANDS + band, plane * BANDS + (band ^ (step * side))))
    return lax.ppermute(block, ("plane", "band"), route)


def coded(values, power):
    row = lax.broadcasted_iota(jnp.int32, values.shape, values.ndim - 2)
    scaled = values * jnp.exp2(TOP - power)
    return jnp.where(row == OWN, power, scaled).astype(jnp.float16)


def power_of(code):
    return code.reshape(-1, SPAN, NROW)[0, OWN : OWN + 1].astype(jnp.float32)


def decoded(code, factor):
    return code.astype(jnp.float32) * factor


def reduced_density(slabs, slot_block, weight):
    far, edges, power = far_sums(slabs, slot_block)
    code = coded(far, power)
    code, later_slots = lax.optimization_barrier((code, slot_block))
    codes = {FAR: exchanged(code, FAR, True)}
    *parts, power = near_sums(slabs, later_slots, edges)
    parts = dict(zip(NEAR, parts))
    for step in NEAR:
        codes[step] = exchanged(coded(parts[step], power), step, True)
    parts[0], _, power, weight = own_sums(slabs, slot_block, weight)
    powers = [power_of(codes[step]) for step in ORDER[:3]]
    power = functools.reduce(jnp.maximum, powers, power)
    factors = {step: jnp.exp2(x - TOP) for step, x in zip(ORDER, powers)}
    sums = {}
    for other in (2, 1, 3, 0):
        total = parts[0][other]
        for step in (3, 1, 2):
            total += decoded(codes[step][other], factors[step])
        sums[other] = total if other == 0 else exchanged(coded(total, power), other, False)
    for other in (2, 1, 3):
        total = sums[0]
        factor = jnp.exp2(power_of(sums[other]) - TOP)
        sums[0] = total + decoded(sums[other], factor)
    return sums[0], weight


def body(slabs, slot_block, lens_weight):
    density, weight = reduced_density(slabs[0], slot_block, lens_weight)
    messages = relaxed(density, weight)
    backwards = [list(range(BANDS))[::-1]]
    rows = lax.all_to_all(
        messages, "band", split_axis=0, concat_axis=0, axis_index_groups=backwards, tiled=True
    )
    rows = rows.reshape(BANDS * MSG, TILE)
    two, one, three = (from_chip(rows, back) for back in (2, 1, 3))
    shape = (6, R, NCOL)
    recent = functools.partial(recent_kernel, 1)
    operands = (rows, from_other_core(rows), one, from_other_core(one))
    recent = chain_call(recent, "chain_recent", operands, shape)
    middle = functools.partial(middle_kernel, 2)
    middle = chain_call(middle, "chain_middle", (two, from_other_core(two)), shape)
    finish = functools.partial(finish_kernel, 3)
    operands = (recent, three, from_other_core(three), middle)
    return chain_call(finish, "chain_finish", operands, (1,) + shape, last=True)


def solution(mesh):
    in_specs = (P("plane", "band", None, None), P("plane", "band"), P("plane"))
    out_specs = P("plane", None, "band", None)
    return jax.shard_map(body, mesh=mesh, in_specs=in_specs, out_specs=out_specs, check_vma=False)
```

```python
import functools

import jax
import jax.numpy as jnp
from jax import lax
from jax.experimental import pallas as pl
from jax.experimental.pallas import tpu as pltpu
from jax.sharding import PartitionSpec as P

NCOL = 8192
NROW = 128
R = 8
BLK = 4
SLOTS = 64
SWEEPS = 20
PLANES = 8
BANDS = 16
SIDE = 4
MASS = 0.05

OWN = NCOL // BANDS
HALO = 20
SPAN = OWN + 2 * HALO
TILE = 128
ROWS = R + 2
MSG = ROWS * OWN // TILE
TOP = 13.0
VMEM_BYTES = 53 * 2**20


FAR, NEAR = 2, (1, 3)
ORDER = (1, 3, 2, 0)


class Relay:
    def __init__(self):
        self.core = lax.rem(lax.axis_index("plane"), 2)
        self.me = lax.axis_index("band")

    def band_at(self, step, other):
        over_y = jnp.where(self.core == 0, other, step)
        over_z = jnp.where(self.core == 0, step, other)
        return self.me ^ (SIDE * over_y + over_z)

    def place(self, band):
        over_y, over_z = (self.me ^ band) // SIDE, (self.me ^ band) % SIDE
        return jnp.where(self.core == 0, SIDE * over_z + over_y, SIDE * over_y + over_z)


def before(band):
    return lax.rem(band + BANDS - 1, BANDS)


def after(band):
    return lax.rem(band + 1, BANDS)


def fill_select(slot_ref, slots, slot_sem, select_ref, turned_ref):
    pltpu.make_async_copy(slot_ref, slots, slot_sem).wait()
    lane = lax.broadcasted_iota(jnp.int32, (8, NROW), 1)
    sub = lax.broadcasted_iota(jnp.int32, (8, NROW), 0)
    picks = []
    for pair in range(SLOTS // 2):
        block = jnp.where(sub < BLK, slots[0, 2 * pair], slots[0, 2 * pair + 1])
        row = block * BLK + (sub & (BLK - 1))
        picks.append(jnp.where(lane == row, 1.0, 0.0))
    select = jnp.concatenate(picks, 0)
    select_ref[...] = select.astype(jnp.bfloat16)
    turned_ref[...] = select.T.astype(jnp.bfloat16)


def summed_turned(slabs, select_ref):
    return lax.dot_general(
        slabs, select_ref[...], (((0,), (0,)), ((), ())), preferred_element_type=jnp.float32
    )


def summed(slabs, turned_ref):
    return jnp.dot(turned_ref[...], slabs, preferred_element_type=jnp.float32)


def larger(most, part):
    return jnp.maximum(most, jnp.max(jnp.abs(part).reshape(-1, 8, NROW), axis=0))


def outer_tiles(slabs):
    return jnp.concatenate([slabs[:, :TILE], slabs[:, -TILE:]], axis=1)


def store_part(out_ref, other, slabs, select_ref, turned_ref, most):
    outer = summed_turned(outer_tiles(slabs), select_ref)
    out_ref[other, 0:TILE] = outer[:TILE]
    out_ref[other, OWN - TILE : OWN] = outer[TILE:]
    inner = summed(slabs[:, TILE : OWN - TILE], turned_ref)
    for tile in range(1, OWN // TILE - 1):
        part = inner[:, (tile - 1) * TILE : tile * TILE]
        out_ref[other, tile * TILE : (tile + 1) * TILE] = part
        most = larger(most, part)
    return outer[:HALO], outer[2 * TILE - HALO :], larger(most, outer)


def power_above(most):
    most = jnp.full((8, NROW), jnp.max(most), jnp.float32)
    return jnp.ceil(jnp.log2(jnp.maximum(most, 2.0**-100)))[0:1]


def window_kernel(step, slot_ref, slab_ref, out_ref, edges_ref, power_ref, *scratch):
    held, select_ref, turned_ref, slots, sems, slot_sem = scratch
    pltpu.make_async_copy(slot_ref, slots, slot_sem).start()
    relay = Relay()

    def fetch(other, act):
        band = relay.band_at(step, other)

        def copy(first, width, to, piece):
            return pltpu.make_async_copy(
                slab_ref.at[:, :, pl.ds(pl.multiple_of(first, TILE), width)],
                held.at[other, :, :, pl.ds(to, width)],
                sems.at[other, piece],
            )

        inside = jnp.logical_and(band > 0, band < BANDS - 1)

        @pl.when(inside)
        def _():
            act(copy(band * OWN - TILE, OWN + 2 * TILE, 0, 0))

        @pl.when(jnp.logical_not(inside))
        def _():
            act(copy(band * OWN, OWN, TILE, 0))
            act(copy(before(band) * OWN + OWN - TILE, TILE, 0, 1))
            act(copy(after(band) * OWN, TILE, TILE + OWN, 2))

    for other in range(SIDE):
        fetch(other, lambda copy: copy.start())
    fill_select(slot_ref, slots, slot_sem, select_ref, turned_ref)

    def chunk(other, most):
        fetch(other, lambda copy: copy.wait())
        slabs = held[other].reshape(SLOTS * BLK, OWN + 2 * TILE)
        low, high, most = store_part(
            out_ref, other, slabs[:, TILE : TILE + OWN], select_ref, turned_ref, most
        )
        edges_ref[other, 0:HALO] = high
        edges_ref[other, HALO:] = low
        outer = summed_turned(outer_tiles(slabs), select_ref)
        left, right = outer[TILE - HALO : TILE], outer[TILE : TILE + HALO]
        out_ref[other, OWN : OWN + HALO] = left
        out_ref[other, OWN + HALO :] = right
        return larger(most, jnp.concatenate([left, right], axis=0))

    most = lax.fori_loop(0, SIDE, chunk, jnp.zeros((8, NROW), jnp.float32))
    power_ref[...] = power_above(most)


def own_kernel(slot_ref, slab_ref, weight_ref, out_ref, edges_ref, power_ref, row_ref, *scratch):
    row_ref[...] = jnp.full((1, NROW), weight_ref[0], jnp.float32)
    window_kernel(0, slot_ref, slab_ref, out_ref, edges_ref, power_ref, *scratch)


def near_kernel(slot_ref, slab_ref, far_edges_ref, *refs):
    out_refs, refs = refs[: len(NEAR)], refs[len(NEAR) :]
    power_ref, held, edges, far_edges, edge_sem, *refs = refs
    select_ref, turned_ref, slots, sems, slot_sem = refs
    pltpu.make_async_copy(slot_ref, slots, slot_sem).start()
    relay = Relay()

    def band_of(slot):
        step = jnp.where(slot < SIDE, NEAR[0], jnp.where(slot < 2 * SIDE, NEAR[1], 0))
        return relay.band_at(step, lax.rem(slot, SIDE))

    def fetch(slot):
        columns = pl.ds(pl.multiple_of(band_of(slot) * OWN, OWN), OWN)
        return pltpu.make_async_copy(slab_ref.at[:, :, columns], held.at[slot], sems.at[slot])

    for slot in range(len(NEAR) * SIDE + SIDE):
        fetch(slot).start()
    fill_select(slot_ref, slots, slot_sem, select_ref, turned_ref)
    far_copy = pltpu.make_async_copy(far_edges_ref, far_edges, edge_sem)
    far_copy.start()

    def chunks(index, most):
        def chunk(other, most):
            slot = SIDE * index + other
            fetch(slot).wait()
            slabs = held[slot].reshape(SLOTS * BLK, OWN)
            low, high, most = store_part(
                out_refs[index], other, slabs, select_ref, turned_ref, most
            )
            edges[relay.place(after(band_of(slot))), 0:HALO] = high
            edges[relay.place(before(band_of(slot))), HALO:] = low
            return most

        return lax.fori_loop(0, SIDE, chunk, most)

    most = jnp.zeros((8, NROW), jnp.float32)
    for index in range(len(NEAR)):
        most = chunks(index, most)

    def rim_chunk(other, carry):
        slot = len(NEAR) * SIDE + other
        fetch(slot).wait()
        band = band_of(slot)
        slabs = held[slot].reshape(SLOTS * BLK, OWN)
        outer = summed_turned(outer_tiles(slabs), select_ref)
        edges[relay.place(after(band)), 0:HALO] = outer[2 * TILE - HALO :]
        edges[relay.place(before(band)), HALO:] = outer[:HALO]
        return carry

    lax.fori_loop(0, SIDE, rim_chunk, 0)
    far_copy.wait()
    for other in range(SIDE):
        band = relay.band_at(FAR, other)
        edges[relay.place(after(band)), 0:HALO] = far_edges[other, 0:HALO]
        edges[relay.place(before(band)), HALO:] = far_edges[other, HALO:]
    for index, step in enumerate(NEAR):
        for other in range(SIDE):
            block = edges[SIDE * step + other]
            out_refs[index][other, OWN:] = block
            most = larger(most, block)
    power_ref[...] = power_above(most)


def sum_call(kernel, name, operands, parts, more, held, sems, third=pltpu.VMEM):
    vmem = pl.BlockSpec(memory_space=pltpu.VMEM)
    return pl.pallas_call(
        kernel,
        in_specs=[pl.BlockSpec(memory_space=pl.ANY)] * 2
        + [pl.BlockSpec(memory_space=third)] * (len(operands) - 2),
        out_specs=[vmem] * (parts + len(more)),
        out_shape=[pltpu.VMEM((SIDE, SPAN, NROW), jnp.float32)] * parts + more,
        scratch_shapes=held
        + [
            pltpu.VMEM((SLOTS * BLK, NROW), jnp.bfloat16),
            pltpu.VMEM((NROW, SLOTS * BLK), jnp.bfloat16),
            pltpu.SMEM((1, SLOTS), jnp.int32),
            pltpu.SemaphoreType.DMA(sems),
            pltpu.SemaphoreType.DMA,
        ],
        compiler_params=pltpu.CompilerParams(vmem_limit_bytes=VMEM_BYTES),
        name=name,
    )(*operands)


POWER = pltpu.VMEM((1, NROW), jnp.float32)
EDGES = pltpu.VMEM((BANDS, 2 * HALO, NROW), jnp.float32)


FAR_EDGES = pltpu.VMEM((SIDE, 2 * HALO, NROW), jnp.float32)
WINDOW = pltpu.VMEM((SIDE, SLOTS, BLK, OWN + 2 * TILE), jnp.bfloat16)


def far_sums(slabs, slot_block):
    kernel = functools.partial(window_kernel, FAR)
    more = [FAR_EDGES, POWER]
    return sum_call(kernel, "far_sums", (slot_block, slabs), 1, more, [WINDOW], (SIDE, 3))


def own_sums(slabs, slot_block, weight):
    operands = (slot_block, slabs, weight)
    more = [FAR_EDGES, POWER, POWER]
    return sum_call(own_kernel, "own_sums", operands, 1, more, [WINDOW], (SIDE, 3), pltpu.SMEM)


def near_sums(slabs, slot_block, edges):
    count = SIDE * len(NEAR) + SIDE
    held = pltpu.VMEM((count, SLOTS, BLK, OWN), jnp.bfloat16)
    operands = (slot_block, slabs, edges)
    scratch = [held, EDGES, FAR_EDGES, pltpu.SemaphoreType.DMA]
    return sum_call(near_kernel, "near_sums", operands, 2, [POWER], scratch, (count,), pl.ANY)


STEPS = SPAN // 8


def relax_kernel(weight_ref, part_ref, out_ref, plain_ref, density_ref, even_ref, odd_ref, turned_ref):
    zero = jnp.zeros((8, NROW), jnp.float32)
    turned_ref[0:8] = zero
    turned_ref[8 + NROW :] = zero
    lane = lax.broadcasted_iota(jnp.int32, (8, NROW), 1)
    not_first = lane > 0
    not_last = lane < NROW - 1
    share = 1.0 / (4.0 + MASS)

    plain_ref[0:HALO] = part_ref[OWN : OWN + HALO]
    plain_ref[HALO + OWN :] = part_ref[OWN + HALO :]
    for tile in range(OWN // TILE):
        part = part_ref[tile * TILE : (tile + 1) * TILE]
        part = part if tile in (0, OWN // TILE - 1) else part.T
        plain_ref[HALO + tile * TILE : HALO + (tile + 1) * TILE] = part

    for t in range(STEPS):
        block = plain_ref[pl.ds(t, 8, stride=STEPS)]
        density_ref[8 * t : 8 * t + 8] = block
        even_ref[8 * t : 8 * t + 8] = block * share

    def sweep(src, dst):
        first = here = src[0:8]
        behind = pltpu.roll(src[8 * STEPS - 8 :], 1, 0)
        for t in range(STEPS):
            ahead = src[8 * t + 8 : 8 * t + 16] if t < STEPS - 1 else pltpu.roll(first, 7, 0)
            total = behind + ahead + density_ref[8 * t : 8 * t + 8]
            total += jnp.where(not_first, pltpu.roll(here, 1, 1), 0.0)
            total += jnp.where(not_last, pltpu.roll(here, NROW - 1, 1), 0.0)
            dst[8 * t : 8 * t + 8] = total * share
            behind, here = here, ahead

    def two_sweeps(_, carry):
        sweep(even_ref, odd_ref)
        sweep(odd_ref, even_ref)
        return carry

    lax.fori_loop(0, (SWEEPS - 1) // 2, two_sweeps, 0)
    sweep(even_ref, odd_ref)
    weight = jnp.broadcast_to(weight_ref[...], (8, NROW))
    for t in range(STEPS):
        plain_ref[pl.ds(t, 8, stride=STEPS)] = odd_ref[8 * t : 8 * t + 8] * weight
    for tile in range(OWN // TILE):
        first = HALO + tile * TILE
        turned_ref[8 : 8 + NROW] = plain_ref[first : first + TILE].T
        for band in range(BANDS):
            out_ref[BANDS - 1 - band, tile * ROWS : (tile + 1) * ROWS] = turned_ref[
                R * band + 7 : R * band + 7 + ROWS
            ]


def relaxed(density, weight):
    return pl.pallas_call(
        relax_kernel,
        in_specs=[
            pl.BlockSpec(memory_space=pltpu.VMEM),
            pl.BlockSpec(memory_space=pltpu.VMEM),
        ],
        out_specs=pl.BlockSpec(memory_space=pltpu.VMEM),
        out_shape=jax.ShapeDtypeStruct((BANDS, MSG, TILE), jnp.float32),
        scratch_shapes=[
            pltpu.VMEM((SPAN, NROW), jnp.float32),
            pltpu.VMEM((SPAN, NROW), jnp.float32),
            pltpu.VMEM((SPAN, NROW), jnp.float32),
            pltpu.VMEM((SPAN, NROW), jnp.float32),
            pltpu.VMEM((NROW + 16, TILE), jnp.float32),
        ],
        compiler_params=pltpu.CompilerParams(vmem_limit_bytes=24 * 2**20),
        name="relaxed",
    )(weight, density)


GROUP = OWN // TILE
PART = NCOL // SIDE


def plane_maps(ref, starts, is_first, is_last):
    mid, rise, both = [], [], []
    for start in starts:
        south, north = ref[pl.ds(start, R)], ref[pl.ds(start + 2, R)]
        mid.append(ref[pl.ds(start + 1, R)])
        rise.append(north - south)
        both.append(north + south)
    easts = [[pltpu.roll(x, TILE - 1, 1) for x in xs[1:]] for xs in (mid, rise)]
    wests = [[pltpu.roll(x, 1, 1) for x in xs[:-1]] for xs in (mid, rise)]
    maps = []
    for t in range(GROUP):
        east, rise_east = (jnp.where(is_last, e[t + 1], e[t]) for e in easts)
        west, rise_west = (jnp.where(is_first, w[t], w[t + 1]) for w in wests)
        twice = 2.0 * mid[t + 1]
        p11 = 1.0 - (east - twice + west)
        p22 = 1.0 - (both[t + 1] - twice)
        p12 = 0.25 * (rise_west - rise_east)
        maps.append((p11, p12, p22, 0.5 * (east - west), 0.5 * rise[t + 1]))
    return maps


def after_map(state, maps):
    a11, a12, a21, a22, s1, s2 = state
    p11, p12, p22, c1, c2 = maps
    return (
        a11 * p11 + a12 * p12,
        a11 * p12 + a12 * p22,
        a21 * p11 + a22 * p12,
        a21 * p12 + a22 * p22,
        a11 * c1 + a12 * c2 + s1,
        a21 * c1 + a22 * c2 + s2,
    )


def after_state(state, first):
    a11, a12, a21, a22, s1, s2 = state
    b11, b12, b21, b22, t1, t2 = first
    return (
        a11 * b11 + a12 * b21,
        a11 * b12 + a12 * b22,
        a21 * b11 + a22 * b21,
        a21 * b12 + a22 * b22,
        a11 * t1 + a12 * t2 + s1,
        a21 * t1 + a22 * t2 + s2,
    )


def chain_step(state_ref, out_ref, pieces, middle_ref=None, final_ref=None, sems=None):
    lane = lax.broadcasted_iota(jnp.int32, (R, TILE), 1)
    is_first = lane == 0
    is_last = lane == TILE - 1

    def group_body(group, carry):
        here = pl.multiple_of(group * MSG, 8)
        behind = pl.multiple_of(lax.rem(group + 1, BANDS) * MSG, 8)
        ahead = pl.multiple_of(lax.rem(group + BANDS - 1, BANDS) * MSG, 8)
        starts = [behind + MSG - ROWS] + [here + t * ROWS for t in range(GROUP)] + [ahead]
        first = (BANDS - 1 - group) * OWN
        columns = [pl.ds(pl.multiple_of(first + t * TILE, TILE), TILE) for t in range(GROUP)]
        maps = [plane_maps(piece, starts, is_first, is_last) for piece in pieces]
        for t in range(GROUP):
            if state_ref is None:
                p11, p12, p22, c1, c2 = maps[0][t]
                state = (p11, p12, p12, p22, c1, c2)
                rest = maps[1:]
            else:
                state = tuple(state_ref[entry, :, columns[t]] for entry in range(6))
                rest = maps
            if middle_ref is not None:
                middle = [middle_ref[entry, :, columns[t]] for entry in range(6)]
                state = after_state(state, middle)
            for one in rest:
                state = after_map(state, one[t])
            if final_ref is not None:
                state = tuple(x - 1.0 if e in (0, 3) else x for e, x in enumerate(state))
            for entry in range(6):
                out_ref[entry, :, columns[t]] = state[entry]
        return carry

    def columns_of(part):
        return pl.ds(pl.multiple_of(part * PART, PART), PART)

    def copy_out(part):
        columns = columns_of(part)
        return pltpu.make_async_copy(
            out_ref.at[:, :, columns], final_ref.at[:, :, columns], sems.at[part]
        )

    def part_body(part, carry):
        for group in range(SIDE):
            group_body(part * SIDE + group, 0)
        if final_ref is not None:
            copy_out(SIDE - 1 - part).start()
        return carry

    lax.fori_loop(0, SIDE, part_body, 0)
    if final_ref is not None:
        for part in range(SIDE):
            copy_out(part).wait()


def recent_kernel(back, own_ref, other_ref, one_ref, one_other_ref, out_ref):
    me = lax.axis_index("plane")
    chip, core = me // 2, lax.rem(me, 2)
    for which in (0, 1):
        near = [own_ref, other_ref] if which else [own_ref]
        far = [one_ref, one_other_ref] if which else [one_other_ref, one_ref]

        @pl.when(jnp.logical_and(chip < back, core == which))
        def _():
            chain_step(None, out_ref, near)

        @pl.when(jnp.logical_and(chip >= back, core == which))
        def _():
            chain_step(None, out_ref, near + far)


def middle_kernel(back, own_ref, other_ref, out_ref):
    me = lax.axis_index("plane")
    chip, core = me // 2, lax.rem(me, 2)
    for which in (0, 1):
        pieces = [own_ref, other_ref] if which else [other_ref, own_ref]

        @pl.when(jnp.logical_and(chip >= back, core == which))
        def _():
            chain_step(None, out_ref, pieces)


def finish_kernel(back, state_ref, own_ref, other_ref, middle_ref, final_ref, out_ref, sems):
    me = lax.axis_index("plane")
    chip, core = me // 2, lax.rem(me, 2)
    final_ref = final_ref.at[0]

    @pl.when(chip < back - 1)
    def _():
        chain_step(state_ref, out_ref, [], None, final_ref, sems)

    @pl.when(chip == back - 1)
    def _():
        chain_step(state_ref, out_ref, [], middle_ref, final_ref, sems)

    for which in (0, 1):
        pieces = [own_ref, other_ref] if which else [other_ref, own_ref]

        @pl.when(jnp.logical_and(chip >= back, core == which))
        def _():
            chain_step(state_ref, out_ref, pieces, middle_ref, final_ref, sems)


def chain_call(kernel, name, operands, shape, last=False):
    vmem = pl.BlockSpec(memory_space=pltpu.VMEM)
    scratch = [pltpu.VMEM((6, R, NCOL), jnp.float32), pltpu.SemaphoreType.DMA((SIDE,))]
    return pl.pallas_call(
        kernel,
        in_specs=[vmem] * len(operands),
        out_specs=pl.BlockSpec(memory_space=pl.ANY) if last else vmem,
        scratch_shapes=scratch if last else [],
        out_shape=jax.ShapeDtypeStruct(shape, jnp.float32),
        cost_estimate=pl.CostEstimate(
            flops=80 * R * NCOL,
            bytes_accessed=sum(4 * x.size for x in operands) + 24 * R * NCOL,
            transcendentals=0,
        ),
        compiler_params=pltpu.CompilerParams(vmem_limit_bytes=16 * 2**20),
        name=name,
    )(*operands)


def from_chip(block, back):
    return lax.ppermute(block, "plane", [(i, (i + 2 * back) % PLANES) for i in range(PLANES)])


def from_other_core(block):
    return lax.ppermute(block, "plane", [(i, i ^ 1) for i in range(PLANES)])


def exchanged(block, step, first):
    route = []
    for plane in range(PLANES):
        side = 1 if (plane % 2 == 0) == first else SIDE
        for band in range(BANDS):
            route.append((plane * BANDS + band, plane * BANDS + (band ^ (step * side))))
    return lax.ppermute(block, ("plane", "band"), route)


def coded(values, power):
    row = lax.broadcasted_iota(jnp.int32, values.shape, values.ndim - 2)
    scaled = values * jnp.exp2(TOP - power)
    return jnp.where(row == OWN, power, scaled).astype(jnp.float16)


def power_of(code):
    return code.reshape(-1, SPAN, NROW)[0, OWN : OWN + 1].astype(jnp.float32)


def decoded(code, factor):
    return code.astype(jnp.float32) * factor


def reduced_density(slabs, slot_block, weight):
    far, edges, power = far_sums(slabs, slot_block)
    code = coded(far, power)
    code, later_slots = lax.optimization_barrier((code, slot_block))
    codes = {FAR: exchanged(code, FAR, True)}
    *parts, power = near_sums(slabs, later_slots, edges)
    parts = dict(zip(NEAR, parts))
    for step in NEAR:
        codes[step] = exchanged(coded(parts[step], power), step, True)
    parts[0], _, power, weight = own_sums(slabs, slot_block, weight)
    powers = [power_of(codes[step]) for step in ORDER[:3]]
    power = functools.reduce(jnp.maximum, powers, power)
    factors = {step: jnp.exp2(x - TOP) for step, x in zip(ORDER, powers)}
    sums = {}
    for other in (2, 1, 3, 0):
        total = parts[0][other]
        for step in (3, 1, 2):
            total += decoded(codes[step][other], factors[step])
        sums[other] = total if other == 0 else exchanged(coded(total, power), other, False)
    for other in (2, 1, 3):
        total = sums[0]
        factor = jnp.exp2(power_of(sums[other]) - TOP)
        sums[0] = total + decoded(sums[other], factor)
    return sums[0], weight


def body(slabs, slot_block, lens_weight):
    density, weight = reduced_density(slabs[0], slot_block, lens_weight)
    messages = relaxed(density, weight)
    backwards = [list(range(BANDS))[::-1]]
    rows = lax.all_to_all(
        messages, "band", split_axis=0, concat_axis=0, axis_index_groups=backwards, tiled=True
    )
    rows = rows.reshape(BANDS * MSG, TILE)
    two, one, three = (from_chip(rows, back) for back in (2, 1, 3))
    shape = (6, R, NCOL)
    recent = functools.partial(recent_kernel, 1)
    operands = (rows, from_other_core(rows), one, from_other_core(one))
    recent = chain_call(recent, "chain_recent", operands, shape)
    middle = functools.partial(middle_kernel, 2)
    middle = chain_call(middle, "chain_middle", (two, from_other_core(two)), shape)
    finish = functools.partial(finish_kernel, 3)
    operands = (recent, three, from_other_core(three), middle)
    return chain_call(finish, "chain_finish", operands, (1,) + shape, last=True)


def solution(mesh):
    in_specs = (P("plane", "band", None, None), P("plane", "band"), P("plane"))
    out_specs = P("plane", None, "band", None)
    return jax.shard_map(body, mesh=mesh, in_specs=in_specs, out_specs=out_specs, check_vma=False)
```
